128 devices in a mesh: grp: 4 (over y), leaf: 32 (over x, z, core).
Axes of the slice: x: 4, y: 4, z: 4, core: 2. Of those that a mesh axis runs over, the one named last changes fastest.
Arguments:
- right_side: float32 [98304, 512], P(('grp', 'leaf')), may hold values from -6 to 6
- guess: float32 [98304, 512], P(('grp', 'leaf')), may hold values from -6 to 6
- near_diag: float32 [128, 768, 768], P(('grp', 'leaf')), as said below
- near_lower: float32 [128, 768, 768], P(('grp', 'leaf')), may hold values from -0.0546875 to 0.0546875
- near_upper: float32 [128, 768, 768], P(('grp', 'leaf')), may hold values from -0.0546875 to 0.0546875
- leaf_inverse: float32 [128, 768, 768], P(('grp', 'leaf')), as said below
- leaf_basis: float32 [128, 768, 128], P(('grp', 'leaf')), may hold values from -0.21875 to 0.21875
- leaf_transfer: float32 [128, 128, 128], P(('grp', 'leaf')), may hold values from -0.5 to 0.5
- mid_share: float32 [128, 128, 128], P(('grp', 'leaf')), may hold values from -0.25 to 0.25
- top_share: float32 [128, 128, 128], P(('grp', 'leaf')), may hold values from -0.09375 to 0.09375
- coupling_share: float32 [128, 3, 128, 128], P(('grp', 'leaf')), as said below
Outputs:
- new_guess: float32 [98304, 512], P(('grp', 'leaf'))
- new_residual: float32 [98304, 512], P(('grp', 'leaf'))
The draws below stay inside these ranges and needn't reach their ends.
Inputs may be any that keep to these rules, and one draw needn't show every extreme that they name: `near_diag`: each leaf's block has a dominant diagonal near 2. `leaf_inverse`: each leaf's matrix is symmetric positive definite. `coupling_share`: every share is symmetric, and each sum of shares that forms a coupling is positive definite.
All inputs are finite; a program needn't handle non-finite values.
Results may differ from the reference program's by a relative error of at most 0.00005.
Values sent between devices are 32-bit elements; how exact they have to be, the bound alone decides.
A program may use at most 128 MiB of HBM per device.

```python
import math
import jax
import jax.numpy as jnp
from jax import lax

LEAF = 768
RANK = 128
RHS = 512
PER_GROUP = 32
LEAVES = 128
ORDER = 98304


def draw_near_diag(key, part):
    own_key = jax.random.fold_in(key, 11)
    noise = jax.random.normal(own_key, (LEAVES, LEAF, LEAF), jnp.float32)
    return 2.0 * jnp.eye(LEAF, dtype=jnp.float32) + noise * (0.5 / math.sqrt(LEAF))


def draw_leaf_inverse(key, part):
    own_key = jax.random.fold_in(key, 23)
    noise = jax.random.normal(own_key, (LEAVES, LEAF, LEAF), jnp.float32)
    symmetric = (noise + jnp.swapaxes(noise, 1, 2)) * (0.25 / math.sqrt(2.0 * LEAF))
    return jnp.eye(LEAF, dtype=jnp.float32) + symmetric


def draw_coupling_share(key, part):
    own_key = jax.random.fold_in(key, 37)
    noise = jax.random.normal(own_key, (LEAVES, 3, RANK, RANK), jnp.float32)
    symmetric = (noise + jnp.swapaxes(noise, 2, 3)) * (0.3 / math.sqrt(2.0 * RANK))
    counts = jnp.array([4.0, PER_GROUP * 1.0, LEAVES * 1.0], jnp.float32).reshape(1, 3, 1, 1)
    return jnp.eye(RANK, dtype=jnp.float32) / counts + symmetric / jnp.sqrt(counts)


def shard_levels(key, shape, split, low, top_value):
    loudness = 1.0
    for dim, shards_of in split:
        heights = jax.random.uniform(jax.random.fold_in(jax.random.fold_in(key, 6), dim), (shards_of,), jnp.float32, low / len(split), top_value / len(split))
        loudness = loudness * jnp.repeat(jnp.exp(heights), shape[dim] // shards_of).reshape((-1,) + (1,) * (len(shape) - 1 - dim))
    return loudness


def gaussian(key, shape, width, bound, split=(), held_as=jnp.bfloat16):
    values = width * jax.random.normal(key, shape, jnp.float32)
    if split:
        values = values * shard_levels(key, shape, split, -0.22, 0.18)
    return jnp.clip(values, -bound, bound).astype(held_as)


def setup_inputs(seed: int = 0) -> dict:
    arg_keys = jax.random.split(jax.random.key(seed), 12)
    right_side = gaussian(arg_keys[0], (ORDER, RHS), 1.0, 6.0, ((0, 128),), jnp.float32)
    guess = gaussian(arg_keys[1], (ORDER, RHS), 1.0, 6.0, ((0, 128),), jnp.float32)
    near_diag = draw_near_diag(jax.random.fold_in(arg_keys[11], 71), 0)
    near_lower = gaussian(arg_keys[3], (LEAVES, LEAF, LEAF), (16 * LEAF) ** -0.5, 0.0546875, ((0, 128),), jnp.float32)
    near_upper = gaussian(arg_keys[4], (LEAVES, LEAF, LEAF), (16 * LEAF) ** -0.5, 0.0546875, ((0, 128),), jnp.float32)
    leaf_inverse = draw_leaf_inverse(jax.random.fold_in(arg_keys[11], 71), 0)
    leaf_basis = gaussian(arg_keys[6], (LEAVES, LEAF, RANK), LEAF ** -0.5, 0.21875, ((0, 128),), jnp.float32)
    leaf_transfer = gaussian(arg_keys[7], (LEAVES, RANK, RANK), RANK ** -0.5, 0.5, ((0, 128),), jnp.float32)
    mid_share = gaussian(arg_keys[8], (LEAVES, RANK, RANK), (4 * RANK) ** -0.5, 0.25, ((0, 128),), jnp.float32)
    top_share = gaussian(arg_keys[9], (LEAVES, RANK, RANK), (PER_GROUP * RANK) ** -0.5, 0.09375, ((0, 128),), jnp.float32)
    coupling_share = draw_coupling_share(jax.random.fold_in(arg_keys[11], 71), 0)
    return {"right_side": right_side, "guess": guess, "near_diag": near_diag, "near_lower": near_lower, "near_upper": near_upper, "leaf_inverse": leaf_inverse, "leaf_basis": leaf_basis, "leaf_transfer": leaf_transfer, "mid_share": mid_share, "top_share": top_share, "coupling_share": coupling_share}


highest = lax.Precision.HIGHEST

def product(left, right):
    return jnp.einsum('...kl,...lr->...kr', left, right, precision=highest)

def across(left, right):
    return jnp.einsum('...kl,...kr->...lr', left, right, precision=highest)

def definite_solve(matrix, target):
    factor = jnp.linalg.cholesky(matrix)
    halfway = lax.linalg.triangular_solve(factor, target, left_side=True, lower=True)
    return lax.linalg.triangular_solve(factor, halfway, left_side=True, lower=True, transpose_a=True)

def near_apply(blocks, near_diag, near_lower, near_upper):
    zero_block = jnp.zeros_like(blocks[:1])
    below_blocks = jnp.concatenate([zero_block, blocks[:-1]], 0)
    above_blocks = jnp.concatenate([blocks[1:], zero_block], 0)
    result = product(near_diag, blocks)
    result = result + product(near_lower, below_blocks)
    return result + product(near_upper, above_blocks)

def by_count(values, group_size):
    return values.reshape((values.shape[0] // group_size, group_size) + values.shape[1:]).sum(1)

def reference(right_side, guess, near_diag, near_lower, near_upper, leaf_inverse, leaf_basis, leaf_transfer, mid_share, top_share, coupling_share):
    blocks_b = right_side.reshape(LEAVES, LEAF, RHS)
    start_x = guess.reshape(LEAVES, LEAF, RHS)
    residual = blocks_b - near_apply(start_x, near_diag, near_lower, near_upper)
    weighted = product(leaf_inverse, leaf_basis)
    leaf_schur = across(leaf_basis, weighted)
    local_sol = product(leaf_inverse, residual)
    reduced = across(leaf_basis, local_sol)
    block_rhs = by_count(across(leaf_transfer, reduced), 4)
    block_proj = by_count(across(leaf_transfer, product(leaf_schur, leaf_transfer)), 4)
    block_mid = by_count(mid_share, 4)
    block_sys = by_count(coupling_share[:, 0], 4) + block_proj
    block_schur = block_proj - product(block_proj, definite_solve(block_sys, block_proj))
    block_red = block_rhs - product(block_proj, definite_solve(block_sys, block_rhs))
    node_count = PER_GROUP // 4
    group_rhs = by_count(across(block_mid, block_red), node_count)
    group_proj = by_count(across(block_mid, product(block_schur, block_mid)), node_count)
    group_top = by_count(top_share, PER_GROUP)
    group_sys = by_count(coupling_share[:, 1], PER_GROUP) + group_proj
    group_schur = group_proj - product(group_proj, definite_solve(group_sys, group_proj))
    group_red = group_rhs - product(group_proj, definite_solve(group_sys, group_rhs))
    root_rhs = across(group_top, group_red).sum(0)
    root_proj = across(group_top, product(group_schur, group_top)).sum(0)
    root_sys = coupling_share[:, 2].sum(0) + root_proj
    root_t = definite_solve(root_sys, root_rhs)
    group_in = product(group_top, root_t[None])
    group_out = group_in + definite_solve(group_sys, group_rhs - product(group_proj, group_in))
    block_in = product(block_mid, jnp.repeat(group_out, node_count, 0))
    block_out = block_in + definite_solve(block_sys, block_rhs - product(block_proj, block_in))
    leaf_in = product(leaf_transfer, jnp.repeat(block_out, 4, 0))
    new_blocks = start_x + (local_sol - product(weighted, leaf_in))
    new_resid = blocks_b - near_apply(new_blocks, near_diag, near_lower, near_upper)
    return (new_blocks.reshape(ORDER, RHS), new_resid.reshape(ORDER, RHS))
```

```python
import jax
import jax.numpy as jnp
from jax import lax
from jax.experimental import pallas as pl
from jax.experimental.pallas import tpu as pltpu
from jax.sharding import PartitionSpec as P

MESH = pl.DeviceIdType.MESH
F32 = jnp.float32
BF16 = jnp.bfloat16
LEAF, RANK, RHS = 768, 128, 512
HALF = RHS // 2


def dot(left, right, over=(1, 0)):
    return lax.dot_general(
        left,
        right,
        (((over[0],), (over[1],)), ((), ())),
        precision=lax.Precision.HIGHEST,
        preferred_element_type=F32,
    )


def split(value):
    high = value.astype(BF16)
    return high, (value - high.astype(F32)).astype(BF16)


def plain(left, right, over=(1, 0)):
    return lax.dot_general(
        left, right, (((over[0],), (over[1],)), ((), ())), preferred_element_type=F32
    )


def stacked(pair_ref, value):
    count = pair_ref.shape[0] // 2
    high, low = split(value)
    both = plain(pair_ref[...], high)
    return both[:count] + both[count:] + plain(pair_ref[:count], low)


def spd_inverse(a):
    lane = lax.broadcasted_iota(jnp.int32, (8, 128), 1)
    sub = lax.broadcasted_iota(jnp.int32, (8, 128), 0)
    head = lane < 8
    unit = jnp.where(lane == sub, -1.0, 0.0)

    def step(_, rows):
        p = rows[0]
        sc = {}
        for i in range(8):
            for k in range(i, 8):
                sc[i, k] = jnp.broadcast_to(p[i:i + 1, k:k + 1], (8, 128))
        get = lambda i, k: sc[min(i, k), max(i, k)]
        for q in range(0, 8, 2):
            aa, bb, cc = sc[q, q], sc[q, q + 1], sc[q + 1, q + 1]
            inv = 1.0 / (aa * cc - bb * bb)
            ia, ib, ic = cc * inv, -bb * inv, aa * inv
            others = [i for i in range(8) if i not in (q, q + 1)]
            p0 = {i: get(i, q) for i in others}
            p1 = {i: get(i, q + 1) for i in others}
            q0 = {i: ia * p0[i] + ib * p1[i] for i in others}
            q1 = {i: ib * p0[i] + ic * p1[i] for i in others}
            for i in others:
                for k in others:
                    if i <= k:
                        sc[i, k] = sc[i, k] - (p0[i] * q0[k] + p1[i] * q1[k])
            for i in others:
                sc[min(i, q), max(i, q)] = q0[i]
                sc[min(i, q + 1), max(i, q + 1)] = q1[i]
            sc[q, q], sc[q, q + 1], sc[q + 1, q + 1] = -ia, -ib, -ic
        pm = jnp.where(head, unit, p)
        pb = [jnp.broadcast_to(pm[m:m + 1, :], (8, 128)) for m in range(8)]
        nq = []
        for k in range(8):
            t = get(k, 0) * pb[0]
            for m in range(1, 8):
                t = t + get(k, m) * pb[m]
            nq.append(t)
        out = []
        for i in range(1, 16):
            r = rows[i]
            t = jnp.where(head, 0.0, r)
            for k in range(8):
                t = t + jnp.broadcast_to(r[:, k:k + 1], (8, 128)) * nq[k]
            out.append(pltpu.roll(t, 120, 1))
        t = nq[7]
        for k in range(7):
            t = jnp.where(sub == k, nq[k], t)
        out.append(pltpu.roll(-t, 120, 1))
        return tuple(out)

    rows = tuple(a[8 * i:8 * i + 8, :] for i in range(16))
    rows = lax.fori_loop(0, 16, step, rows)
    return -jnp.concatenate(rows, 0)

def tree_kernel(
    right_h,
    guess_h,
    diag_h,
    lower_h,
    upper_h,
    inverse_h,
    basis_h,
    trans_h,
    mid_h,
    top_h,
    coup_h,
    base_o,
    left_o,
    out_o,
    cross_o,
    node_o,
    wide,
    pairs,
    right,
    guess,
    resid,
    sol,
    base,
    halo,
    halo2,
    basis,
    trans,
    expand,
    expand_halo,
    project,
    share,
    proj,
    e1s,
    e1p,
    three,
    node_m,
    xs_out,
    xs_in,
    zs_out,
    zs_in,
    group_m,
    q_out,
    xq_in,
    zq_out,
    zq_in,
    gp_out,
    root_out,
    root_in,
    reduced,
    r1_in,
    v_out,
    r2_in,
    u_out,
    r3_in,
    gout,
    block_own,
    block_out,
    block_halo,
    load_sem,
    store_sem,
    send_sem,
    recv_sem,
):
    y = lax.axis_index("grp")
    l = lax.axis_index("leaf")
    j = l % 4
    node = l // 4
    first = l - j
    index = y * 32 + l

    def at(place):
        place = place % 128
        return (place // 32, place % 32)

    nxt, prv = at(index + 1), at(index + 127)
    spots = [(j + d) % 4 for d in (1, 2, 3)]
    mates = [(y, first + spot) for spot in spots]
    cross = [(y, (l + 8 * d) % 32) for d in (1, 2, 3)]
    across_z = (y, l + 4 - 8 * (node % 2))
    peers = [(y, (l + 4 * d) % 32) for d in range(1, 8)]
    peer_spots = [(node + d) % 8 for d in range(1, 8)]
    ring = [((y + d) % 4, l) for d in (1, 2, 3)]

    counter = [0]
    sent = []

    def remote(src, dst, device, start=True):
        k = counter[0]
        counter[0] += 1
        copy = pltpu.make_async_remote_copy(
            src_ref=src,
            dst_ref=dst,
            send_sem=send_sem.at[k],
            recv_sem=recv_sem.at[k],
            device_id=device,
            device_id_type=MESH,
        )
        if start:
            copy.start()
        sent.append(copy)
        return copy

    def arrived(copies):
        for copy in copies:
            copy.wait_recv()

    local = []

    def load(src, dst):
        copy = pltpu.make_async_copy(src, dst, load_sem.at[len(local)])
        copy.start()
        local.append(copy)
        return copy

    load_share = [
        load(coup_h, share.at[pl.ds(0, 3)]),
        load(mid_h, share.at[3]),
        load(top_h, share.at[4]),
    ]
    load_inverse = load(inverse_h, wide.at[3])
    load_basis = load(basis_h, basis)
    load_trans = load(trans_h, trans)
    load_guess = load(guess_h, guess)
    load_diag = load(diag_h, wide.at[0])
    load_right = load(right_h, right)
    load_lower = load(lower_h, wide.at[1])
    load_upper = load(upper_h, wide.at[2])

    barrier = pltpu.get_barrier_semaphore()
    for device in [nxt, prv] + mates + peers + ring:
        pl.semaphore_signal(barrier, inc=1, device_id=device, device_id_type=MESH)

    @pl.when(j == 0)
    def _():
        for k in range(4):
            pl.semaphore_signal(
                barrier, inc=1, device_id=at(index + 124 + k), device_id_type=MESH
            )

    @pl.when(j == 3)
    def _():
        for k in range(4):
            pl.semaphore_signal(
                barrier, inc=1, device_id=at(index + 1 + k), device_id_type=MESH
            )

    pl.semaphore_wait(barrier, 17)

    def cols(c):
        return pl.ds(c * HALF, HALF)

    halo_in = []
    for c in range(2):
        halo_in.append(
            [
                remote(guess_h.at[:, cols(c)], halo.at[0, :, cols(c)], nxt),
                remote(guess_h.at[:, cols(c)], halo.at[1, :, cols(c)], prv),
            ]
        )

    for copy in load_share:
        copy.wait()
    e1_static = [
        remote(share.at[:, pl.ds(spots[d] * 32, 32)], e1s.at[d], mates[d]) for d in range(3)
    ]

    def divide(m, scale=None):
        value = wide[m]
        if scale is not None:
            value = value * scale
        high, low = split(value)
        pairs[m, pl.ds(0, LEAF)] = high
        pairs[m, pl.ds(LEAF, LEAF)] = low

    load_inverse.wait()
    load_basis.wait()
    load_trans.wait()
    divide(3)
    basis_t = basis[...].T
    trans_t = trans[...].T
    weighted = dot(wide[3], basis[...])
    expand[...] = dot(weighted, trans[...])
    proj[...] = dot(trans_t, dot(dot(basis_t, weighted), trans[...]))
    e1_proj = [
        remote(proj.at[pl.ds(spots[d] * 32, 32)], e1p.at[d], mates[d]) for d in range(3)
    ]
    expand_in = [
        remote(expand, expand_halo.at[0], nxt),
        remote(expand, expand_halo.at[1], prv),
    ]
    high, low = split(dot(trans_t, basis_t))
    project[pl.ds(0, RANK)] = high
    project[pl.ds(RANK, RANK)] = low

    load_guess.wait()
    load_diag.wait()
    load_right.wait()
    divide(0)

    def own(c, carry):
        here = pl.ds(pl.multiple_of(c * HALF, HALF), HALF)
        resid[:, here] = right[:, here] - stacked(pairs.at[0], guess[:, here])
        return carry

    lax.fori_loop(0, 2, own, 0)

    rows = pl.ds(pl.multiple_of(j * 32, 32), 32)
    arrived(e1_static)
    sums = share[:, rows] + e1s[0] + e1s[1] + e1s[2]
    xs_out[0:2] = sums[1:3]
    xs_out[2] = sums[4]
    xs_copies = [remote(xs_out, xs_in.at[d], cross[d]) for d in range(3)]
    arrived(e1_proj)
    three[0] = proj[rows] + e1p[0] + e1p[1] + e1p[2]
    three[1] = sums[0]
    three[2] = sums[3]
    node_m[:, rows] = three[...]
    e2 = [remote(three, node_m.at[:, rows], mates[d]) for d in range(3)]

    load_lower.wait()
    load_upper.wait()
    divide(1, jnp.where(index == 0, 0.0, 1.0))
    divide(2, jnp.where(index == 127, 0.0, 1.0))

    arrived(xs_copies)
    zs_out[...] = xs_out[...] + xs_in[0] + xs_in[1] + xs_in[2]
    zs_copy = remote(zs_out, zs_in, across_z)

    arrived(e2)
    p_proj, p_coup, p_mid = node_m[0], node_m[1], node_m[2]
    p_inv = spd_inverse(p_proj + p_coup)
    fm = dot(dot(p_inv, p_coup), p_mid)
    mf = fm.T
    q_node = dot(mf, dot(p_proj, p_mid))
    q_out[...] = q_node
    xq_copies = [remote(q_out.at[rows], xq_in.at[d], cross[d]) for d in range(3)]

    arrived([zs_copy])
    gstat = zs_out[...] + zs_in[...]
    xs_sum = gstat
    group_m[pl.ds(0, 3), rows] = xs_sum
    e4_static = [
        remote(group_m.at[pl.ds(0, 3), rows], group_m.at[pl.ds(0, 3), rows], mates[d])
        for d in range(3)
    ]

    def leaf_chunk(c):
        here = cols(c)
        arrived(halo_in[c])

        def side(k, carry):
            resid[:, here] = resid[:, here] - stacked(pairs.at[k + 1], halo[k, :, here])
            return carry

        lax.fori_loop(0, 2, side, 0)
        sol[:, here] = stacked(pairs.at[3], resid[:, here])
        return [
            remote(sol.at[:, here], halo2.at[0, :, here], nxt),
            remote(sol.at[:, here], halo2.at[1, :, here], prv),
        ]

    def reduce_chunk(c):
        here = cols(c)
        reduced[here, :] = stacked(project, sol[:, here]).T
        base[:, here] = guess[:, here] + sol[:, here]

    halo2_in = [leaf_chunk(0)]

    arrived(xq_copies)
    zq_out[...] = q_out[rows] + xq_in[0] + xq_in[1] + xq_in[2]
    zq_copy = remote(zq_out, zq_in, across_z)
    reduce_chunk(0)

    arrived([zq_copy])
    gp_out[...] = zq_out[...] + zq_in[...]
    group_m[3, rows] = gp_out[...]
    e4 = [remote(gp_out, group_m.at[3, rows], mates[d]) for d in range(3)]

    halo2_in.append(leaf_chunk(1))
    reduce_chunk(1)
    r1_copies = [
        remote(reduced.at[pl.ds(spots[d] * 128, 128)], r1_in.at[d], mates[d]) for d in range(3)
    ]

    arrived(e4_static)
    arrived(e4)
    g_coup, r_coup, g_top, g_proj = group_m[0], group_m[1], group_m[2], group_m[3]
    g_inv = spd_inverse(g_proj + g_coup)
    gf_t = dot(g_inv, g_coup)
    ft = dot(gf_t, g_top)
    ft_t = ft.T
    root_out[...] = r_coup + dot(ft_t, dot(g_proj, g_top))
    root_copies = [remote(root_out, root_in.at[d], ring[d]) for d in range(3)]

    arrived(r1_copies)
    wide_rows = pl.ds(pl.multiple_of(j * 128, 128), 128)
    block_rhs = reduced[wide_rows] + r1_in[0] + r1_in[1] + r1_in[2]
    v_out[...] = dot(block_rhs, fm)
    r2_copies = [
        remote(v_out.at[pl.ds(peer_spots[d] * 16, 16)], r2_in.at[d], peers[d]) for d in range(7)
    ]
    block_part = dot(block_rhs, p_inv)

    def again(c, carry):
        here = pl.ds(pl.multiple_of(c * HALF, HALF), HALF)
        resid[:, here] = resid[:, here] - stacked(pairs.at[0], sol[:, here])
        return carry

    lax.fori_loop(0, 2, again, 0)
    arrived(expand_in)
    cross_o[:, pl.ds(0, RANK)] = stacked(pairs.at[0], expand[...])
    for k in range(2):
        cross_o[:, pl.ds((k + 1) * RANK, RANK)] = stacked(pairs.at[k + 1], expand_halo[k])
    out_o[...] = expand[...]

    arrived(r2_copies)
    few_rows = pl.ds(pl.multiple_of(node * 16, 16), 16)
    group_rhs = v_out[few_rows]
    for d in range(7):
        group_rhs = group_rhs + r2_in[d]
    u_out[...] = dot(group_rhs, ft)
    r3_copies = [remote(u_out, r3_in.at[d], ring[d]) for d in range(3)]
    group_part = dot(group_rhs, g_inv)

    arrived(root_copies)
    r_inv = spd_inverse(root_out[...] + root_in[0] + root_in[1] + root_in[2])
    down = dot(r_inv, ft_t)

    arrived(r3_copies)
    root_rhs = u_out[...] + r3_in[0] + r3_in[1] + r3_in[2]
    gout[few_rows] = group_part + dot(root_rhs, down)
    r4_copies = [remote(gout.at[few_rows], gout.at[few_rows], peers[d]) for d in range(7)]

    for c in range(2):
        here = cols(c)
        arrived(halo2_in[c])

        def side2(k, carry):
            resid[:, here] = resid[:, here] - stacked(pairs.at[k + 1], halo2[k, :, here])
            return carry

        lax.fori_loop(0, 2, side2, 0)

    stores = [
        pltpu.make_async_copy(base, base_o, store_sem.at[0]),
        pltpu.make_async_copy(resid, left_o, store_sem.at[1]),
    ]
    for copy in stores:
        copy.start()

    arrived(r4_copies)
    block_own[...] = block_part + dot(gout[...], mf)
    block_out[wide_rows] = block_own[...]
    r5_copies = [remote(block_own, block_out.at[wide_rows], mates[d]) for d in range(3)]
    k5 = counter[0]
    ahead = [at(index - j + 4), at(index - j + 127)]
    extra = [
        pltpu.make_async_remote_copy(
            src_ref=block_own,
            dst_ref=block_halo.at[wide_rows],
            send_sem=send_sem.at[k5 + way],
            recv_sem=recv_sem.at[k5 + 2 + j],
            device_id=ahead[way],
            device_id_type=MESH,
        )
        for way in range(2)
    ]
    for copy in extra:
        copy.start()

    arrived(r5_copies)
    for k in range(3):
        node_o[:, pl.ds(k * RANK, RANK)] = block_out[...]

    def from_halo(k):
        for spot in range(4):
            pltpu.make_async_remote_copy(
                src_ref=block_own,
                dst_ref=block_halo.at[pl.ds(spot * 128, 128)],
                send_sem=send_sem.at[k5],
                recv_sem=recv_sem.at[k5 + 2 + spot],
                device_id=ahead[0],
                device_id_type=MESH,
            ).wait_recv()
        node_o[:, pl.ds(k * RANK, RANK)] = block_halo[...]

    @pl.when(j == 0)
    def _():
        from_halo(1)

    @pl.when(j == 3)
    def _():
        from_halo(2)

    for copy in sent:
        copy.wait_send()
    for copy in extra:
        copy.wait_send()
    for copy in stores:
        copy.wait()


def last_kernel(base_ref, left_ref, out_ref, cross_ref, node_ref, guess_ref, resid_ref):
    def three(left, right):
        left_high, left_low = split(left)
        right_high, right_low = split(right)
        over = (1, 1)
        return (
            plain(left_high, right_high, over)
            + plain(left_low, right_high, over)
            + plain(left_high, right_low, over)
        )

    node = node_ref[...]
    guess_ref[...] = base_ref[...] - three(out_ref[...], node[:, :RANK])
    resid_ref[...] = left_ref[...] + three(cross_ref[...], node)


def tree(*args):
    any_spec = pl.BlockSpec(memory_space=pl.ANY)
    vmem = pl.BlockSpec(memory_space=pltpu.VMEM)

    def buf(*shape, dtype=F32):
        return pltpu.VMEM(shape, dtype)

    scratch = [
        buf(4, LEAF, LEAF),
        buf(4, 2 * LEAF, LEAF, dtype=BF16),
        buf(LEAF, RHS),
        buf(LEAF, RHS),
        buf(LEAF, RHS),
        buf(LEAF, RHS),
        buf(LEAF, RHS),
        buf(2, LEAF, RHS),
        buf(2, LEAF, RHS),
        buf(LEAF, RANK),
        buf(RANK, RANK),
        buf(LEAF, RANK),
        buf(2, LEAF, RANK),
        buf(2 * RANK, LEAF, dtype=BF16),
        buf(5, RANK, RANK),
        buf(RANK, RANK),
        buf(3, 5, 32, RANK),
        buf(3, 32, RANK),
        buf(3, 32, RANK),
        buf(3, RANK, RANK),
        buf(3, 32, RANK),
        buf(3, 3, 32, RANK),
        buf(3, 32, RANK),
        buf(3, 32, RANK),
        buf(4, RANK, RANK),
        buf(RANK, RANK),
        buf(3, 32, RANK),
        buf(32, RANK),
        buf(32, RANK),
        buf(32, RANK),
        buf(RANK, RANK),
        buf(3, RANK, RANK),
        buf(RHS, RANK),
        buf(3, RANK, RANK),
        buf(RANK, RANK),
        buf(7, 16, RANK),
        buf(16, RANK),
        buf(3, 16, RANK),
        buf(RANK, RANK),
        buf(RANK, RANK),
        buf(RHS, RANK),
        buf(RHS, RANK),
        pltpu.SemaphoreType.DMA((11,)),
        pltpu.SemaphoreType.DMA((2,)),
        pltpu.SemaphoreType.DMA((72,)),
        pltpu.SemaphoreType.DMA((72,)),
    ]
    base, left, out, cross, node = pl.pallas_call(
        tree_kernel,
        out_shape=[
            jax.ShapeDtypeStruct((LEAF, RHS), F32),
            jax.ShapeDtypeStruct((LEAF, RHS), F32),
            jax.ShapeDtypeStruct((LEAF, RANK), F32),
            jax.ShapeDtypeStruct((LEAF, 3 * RANK), F32),
            jax.ShapeDtypeStruct((RHS, 3 * RANK), F32),
        ],
        in_specs=[any_spec] * 11,
        out_specs=[any_spec, any_spec, vmem, vmem, vmem],
        scratch_shapes=scratch,
        compiler_params=pltpu.CompilerParams(
            collective_id=0, has_side_effects=True, vmem_limit_bytes=56 * 2**20
        ),
    )(*args)
    block = 256
    return pl.pallas_call(
        last_kernel,
        grid=(LEAF // block,),
        in_specs=[
            pl.BlockSpec((block, RHS), lambda i: (i, 0)),
            pl.BlockSpec((block, RHS), lambda i: (i, 0)),
            pl.BlockSpec((block, RANK), lambda i: (i, 0)),
            pl.BlockSpec((block, 3 * RANK), lambda i: (i, 0)),
            pl.BlockSpec((RHS, 3 * RANK), lambda i: (0, 0)),
        ],
        out_specs=[
            pl.BlockSpec((block, RHS), lambda i: (i, 0)),
            pl.BlockSpec((block, RHS), lambda i: (i, 0)),
        ],
        out_shape=[jax.ShapeDtypeStruct((LEAF, RHS), F32)] * 2,
    )(base, left, out, cross, node)


def body(
    right_side,
    guess,
    near_diag,
    near_lower,
    near_upper,
    leaf_inverse,
    leaf_basis,
    leaf_transfer,
    mid_share,
    top_share,
    coupling_share,
):
    new_guess, new_residual = tree(
        right_side,
        guess,
        near_diag[0],
        near_lower[0],
        near_upper[0],
        leaf_inverse[0],
        leaf_basis[0],
        leaf_transfer[0],
        mid_share[0],
        top_share[0],
        coupling_share[0],
    )
    return (new_guess, new_residual)


def solution(mesh):
    field = P(("grp", "leaf"), None)
    block = P(("grp", "leaf"), None, None)
    shares = P(("grp", "leaf"), None, None, None)
    in_specs = (field, field) + (block,) * 8 + (shares,)
    return jax.shard_map(
        body, mesh=mesh, in_specs=in_specs, out_specs=(field, field), check_vma=False
    )
```

```python
import jax
import jax.numpy as jnp
from jax import lax
from jax.experimental import pallas as pl
from jax.experimental.pallas import tpu as pltpu
from jax.sharding import PartitionSpec as P

MESH = pl.DeviceIdType.MESH
F32 = jnp.float32
BF16 = jnp.bfloat16
LEAF, RANK, RHS = 768, 128, 512
HALF = RHS // 2


def dot(left, right, over=(1, 0)):
    return lax.dot_general(
        left,
        right,
        (((over[0],), (over[1],)), ((), ())),
        precision=lax.Precision.HIGHEST,
        preferred_element_type=F32,
    )


def split(value):
    high = value.astype(BF16)
    return high, (value - high.astype(F32)).astype(BF16)


def plain(left, right, over=(1, 0)):
    return lax.dot_general(
        left, right, (((over[0],), (over[1],)), ((), ())), preferred_element_type=F32
    )


def stacked(pair_ref, value):
    count = pair_ref.shape[0] // 2
    high, low = split(value)
    both = plain(pair_ref[...], high)
    return both[:count] + both[count:] + plain(pair_ref[:count], low)


def spd_inverse(matrix):
    lane = lax.broadcasted_iota(jnp.int32, (8, 128), 1)
    sub = lax.broadcasted_iota(jnp.int32, (8, 128), 0)

    def total(t):
        return ((t[0] + t[1]) + (t[2] + t[3])) + ((t[4] + t[5]) + (t[6] + t[7]))

    def panel(rows, s):
        at = 8 * s
        head = (lane >= at) & (lane < at + 8)
        p = rows[s]
        sc = {}
        for k in range(8):
            col = jnp.broadcast_to(p[:, at + k : at + k + 1], (8, 128))
            for i in range(k + 1):
                sc[i, k] = jnp.broadcast_to(col[i : i + 1, :], (8, 128))

        def get(i, k):
            return sc[min(i, k), max(i, k)]

        for q in range(0, 8, 2):
            aa, bb, cc = sc[q, q], sc[q, q + 1], sc[q + 1, q + 1]
            det = aa * cc - bb * bb
            inv = pl.reciprocal(det, approx=True)
            inv = inv * (2.0 - det * inv)
            inv = inv * (2.0 - det * inv)
            ia, ib, ic = cc * inv, -bb * inv, aa * inv
            others = [i for i in range(8) if i not in (q, q + 1)]
            p0 = {i: get(i, q) for i in others}
            p1 = {i: get(i, q + 1) for i in others}
            q0 = {i: ia * p0[i] + ib * p1[i] for i in others}
            q1 = {i: ib * p0[i] + ic * p1[i] for i in others}
            for i in others:
                for k in others:
                    if i <= k:
                        sc[i, k] = sc[i, k] - (p0[i] * q0[k] + p1[i] * q1[k])
            for i in others:
                sc[min(i, q), max(i, q)] = q0[i]
                sc[min(i, q + 1), max(i, q + 1)] = q1[i]
            sc[q, q], sc[q, q + 1], sc[q + 1, q + 1] = -ia, -ib, -ic
        pm = jnp.where(head, jnp.where(lane == sub + at, -1.0, 0.0), p)
        pb = [jnp.broadcast_to(pm[m : m + 1, :], (8, 128)) for m in range(8)]
        nq = [total([get(k, m) * pb[m] for m in range(8)]) for k in range(8)]
        out = list(rows)
        for i in [(s + 1 + i) % 16 for i in range(15)]:
            r = rows[i]
            terms = [
                jnp.broadcast_to(r[:, at + k : at + k + 1], (8, 128)) * nq[k] for k in range(8)
            ]
            out[i] = jnp.where(head, 0.0, r) + total(terms)
        t = nq[7]
        for k in range(7):
            t = jnp.where(sub == k, nq[k], t)
        out[s] = -t
        return out

    def step(_, rows):
        rows = list(rows)
        for s in range(4):
            rows = panel(rows, s)
        rows = [pltpu.roll(r, 96, 1) for r in rows]
        return tuple(rows[4:] + rows[:4])

    rows = tuple(matrix[8 * i : 8 * i + 8, :] for i in range(16))
    rows = lax.fori_loop(0, 4, step, rows)
    return -jnp.concatenate(rows, 0)


def tree_kernel(
    right_h,
    guess_h,
    diag_h,
    lower_h,
    upper_h,
    inverse_h,
    basis_h,
    trans_h,
    mid_h,
    top_h,
    coup_h,
    base_o,
    left_o,
    out_o,
    cross_o,
    node_o,
    wide,
    pairs,
    right,
    guess,
    resid,
    sol,
    base,
    halo,
    halo2,
    basis,
    trans,
    expand,
    expand_halo,
    project,
    share,
    proj,
    proj_core,
    proj_z,
    chip,
    chip_in,
    pair_in,
    node_m,
    sx_in,
    sx_out,
    sz_in,
    group_m,
    q_out,
    xq_in,
    zq_out,
    zq_in,
    root_out,
    root_in,
    reduced,
    r1_in,
    v_out,
    r2_in,
    u_out,
    r3_in,
    gout,
    block_own,
    block_out,
    block_halo,
    load_sem,
    store_sem,
    send_sem,
    recv_sem,
):
    y = lax.axis_index("grp")
    l = lax.axis_index("leaf")
    core = l % 2
    j = l % 4
    z = (l // 2) % 4
    x = l // 8
    node = l // 4
    first = l - j
    index = y * 32 + l

    def at(place):
        place = place % 128
        return (place // 32, place % 32)

    nxt, prv = at(index + 1), at(index + 127)
    spots = [(j + d) % 4 for d in (1, 2, 3)]
    mates = [(y, first + spot) for spot in spots]
    twin = (y, l + 1 - 2 * core)
    mate_z = mates[1]
    x_spots = [(x + d) % 4 for d in (1, 2, 3)]
    cross = [(y, (l + 8 * d) % 32) for d in (1, 2, 3)]
    line = [(y, x * 8 + ((z + d) % 4) * 2 + core) for d in (1, 2, 3)]
    across_z = line[1]
    peers = [(y, (l + 4 * d) % 32) for d in range(1, 8)]
    peer_spots = [(node + d) % 8 for d in range(1, 8)]
    ring = [((y + d) % 4, l) for d in (1, 2, 3)]

    counter = [0]
    sent = []

    def remote(src, dst, device, start=True):
        k = counter[0]
        counter[0] += 1
        copy = pltpu.make_async_remote_copy(
            src_ref=src,
            dst_ref=dst,
            send_sem=send_sem.at[k],
            recv_sem=recv_sem.at[k],
            device_id=device,
            device_id_type=MESH,
        )
        if start:
            copy.start()
            sent.append(copy)
        return copy

    def arrived(*copies):
        for copy in copies:
            copy.wait_recv()

    local = []

    def load(src, dst):
        copy = pltpu.make_async_copy(src, dst, load_sem.at[len(local)])
        copy.start()
        local.append(copy)
        return copy

    load_share = [
        load(coup_h.at[0], share.at[0]),
        load(mid_h, share.at[1]),
        load(coup_h.at[pl.ds(1, 2)], share.at[pl.ds(2, 2)]),
        load(top_h, share.at[4]),
    ]
    load_inverse = load(inverse_h, wide.at[3])
    load_basis = load(basis_h, basis)
    load_trans = load(trans_h, trans)
    load_guess = load(guess_h, guess)
    load_diag = load(diag_h, wide.at[0])
    load_right = load(right_h, right)
    load_lower = load(lower_h, wide.at[1])
    load_upper = load(upper_h, wide.at[2])

    barrier = pltpu.get_barrier_semaphore()
    for device in [nxt, prv] + mates + peers + ring + line:
        pl.semaphore_signal(barrier, inc=1, device_id=device, device_id_type=MESH)

    @pl.when(j == 0)
    def _():
        for k in range(4):
            pl.semaphore_signal(
                barrier, inc=1, device_id=at(index + 124 + k), device_id_type=MESH
            )

    @pl.when(j == 3)
    def _():
        for k in range(4):
            pl.semaphore_signal(
                barrier, inc=1, device_id=at(index + 1 + k), device_id_type=MESH
            )

    pl.semaphore_wait(barrier, 20)

    def cols(c):
        return pl.ds(c * HALF, HALF)

    pieces = []

    def add_piece(src, dst, part):
        pieces.append(
            [
                remote(src.at[part], dst.at[(0,) + part], nxt, start=False),
                remote(src.at[part], dst.at[(1,) + part], prv, start=False),
            ]
        )
        return pieces[-1]

    def quarters(src, dst, c):
        return [add_piece(src, dst, (pl.ds(192 * q, 192), cols(c))) for q in range(4)]

    begun = [0]

    def pump(count):
        for _ in range(count):
            k = begun[0]
            if k >= 2:
                for copy in pieces[k - 2]:
                    copy.wait_send()
            for copy in pieces[k]:
                copy.start()
            begun[0] += 1

    halo_in = [quarters(guess_h, halo, c) for c in range(2)]
    expand_in = [
        add_piece(expand, expand_halo, (pl.ds(384 * q, 384), pl.ds(0, RANK))) for q in range(2)
    ]
    halo2_in = [quarters(sol, halo2, c) for c in range(2)]

    pump(2)

    for copy in load_share:
        copy.wait()
    half = pl.ds(pl.multiple_of(core * 64, 64), 64)
    other = pl.ds(pl.multiple_of(64 - core * 64, 64), 64)
    e1 = remote(share.at[:, other], chip_in, twin)

    def divide(m, scale=None):
        value = wide[m]
        if scale is not None:
            value = value * scale
        high, low = split(value)
        pairs[m, pl.ds(0, LEAF)] = high
        pairs[m, pl.ds(LEAF, LEAF)] = low

    load_inverse.wait()
    load_basis.wait()
    load_trans.wait()
    basis_t = basis[...].T
    trans_t = trans[...].T
    weighted = dot(wide[3], basis[...])
    proj[...] = dot(trans_t, dot(dot(basis_t, weighted), trans[...]))
    e_core = remote(proj, proj_core, twin)

    arrived(e1)
    chip[...] = share[:, half] + chip_in[...]
    e_pair = remote(chip.at[pl.ds(0, 2)], pair_in, mate_z)
    sx = [
        remote(chip.at[pl.ds(2, 3), pl.ds(x_spots[d] * 16, 16)], sx_in.at[d], cross[d])
        for d in range(3)
    ]
    arrived(e_core)
    proj_core[...] = proj[...] + proj_core[...]
    e_z = remote(proj_core, proj_z, mate_z)
    pump(2)

    expand[...] = dot(weighted, trans[...])
    high, low = split(dot(trans_t, basis_t))
    project[pl.ds(0, RANK)] = high
    project[pl.ds(RANK, RANK)] = low

    load_guess.wait()
    load_diag.wait()
    load_right.wait()
    divide(0)

    def own(c, carry):
        here = pl.ds(pl.multiple_of(c * HALF, HALF), HALF)
        resid[:, here] = right[:, here] - stacked(pairs.at[0], guess[:, here])
        return carry

    lax.fori_loop(0, 2, own, 0)

    arrived(e_pair)
    node_m[:, half] = chip[0:2] + pair_in[...]
    e_half = remote(node_m.at[:, half], node_m.at[:, half], twin)
    arrived(*sx)
    sx_own = pl.ds(pl.multiple_of(x * 16, 16), 16)
    sx_out[...] = chip[2:5, sx_own] + sx_in[0] + sx_in[1] + sx_in[2]
    sz = [remote(sx_out, sz_in.at[d], line[d]) for d in range(3)]
    arrived(e_z)
    arrived(e_half)
    p_proj, p_coup, p_mid = proj_core[...] + proj_z[...], node_m[0], node_m[1]
    pump(2)
    p_inv = spd_inverse(p_proj + p_coup)
    fm = dot(dot(p_inv, p_coup), p_mid)
    mf = fm.T
    q_out[...] = dot(mf, dot(p_proj, p_mid))
    xq = [remote(q_out.at[half], xq_in.at[d], cross[d]) for d in range(3)]

    arrived(*sz)
    group_rows = pl.ds(pl.multiple_of(core * 64 + x * 16, 16), 16)
    group_m[pl.ds(0, 3), group_rows] = sx_out[...] + sz_in[0] + sz_in[1] + sz_in[2]
    sx2 = [
        remote(group_m.at[pl.ds(0, 3), group_rows], group_m.at[pl.ds(0, 3), group_rows], cross[d])
        for d in range(3)
    ]
    pump(2)

    load_lower.wait()
    load_upper.wait()
    divide(1, jnp.where(index == 0, 0.0, 1.0))
    divide(2, jnp.where(index == 127, 0.0, 1.0))
    divide(3)

    def leaf_chunk(c):
        here = cols(c)
        for pair in halo_in[c]:
            arrived(*pair)

        def side(k, carry):
            resid[:, here] = resid[:, here] - stacked(pairs.at[k + 1], halo[k, :, here])
            return carry

        lax.fori_loop(0, 2, side, 0)
        sol[:, here] = stacked(pairs.at[3], resid[:, here])

    def reduce_chunk(c):
        here = cols(c)
        reduced[here, :] = stacked(project, sol[:, here]).T

    leaf_chunk(0)

    arrived(*xq)
    zq_out[...] = q_out[half] + xq_in[0] + xq_in[1] + xq_in[2]
    zq = remote(zq_out, zq_in, across_z)
    arrived(*sx2)
    s_half = remote(group_m.at[pl.ds(0, 3), half], group_m.at[pl.ds(0, 3), half], twin)
    pump(2)
    reduce_chunk(0)
    base[:, cols(0)] = guess[:, cols(0)] + sol[:, cols(0)]

    arrived(zq)
    group_m[3, half] = zq_out[...] + zq_in[...]
    g_half = remote(group_m.at[3, half], group_m.at[3, half], twin)

    leaf_chunk(1)
    reduce_chunk(1)
    r1 = [remote(reduced.at[pl.ds(spots[d] * 128, 128)], r1_in.at[d], mates[d]) for d in range(3)]
    pump(2)
    base[:, cols(1)] = guess[:, cols(1)] + sol[:, cols(1)]
    base_store = pltpu.make_async_copy(base, base_o, store_sem.at[0])
    base_store.start()

    arrived(s_half, g_half)
    g_coup, r_coup, g_top, g_proj = group_m[0], group_m[1], group_m[2], group_m[3]
    g_inv = spd_inverse(g_proj + g_coup)

    arrived(*r1)
    wide_rows = pl.ds(pl.multiple_of(j * 128, 128), 128)
    block_rhs = reduced[wide_rows] + r1_in[0] + r1_in[1] + r1_in[2]
    v_out[...] = dot(block_rhs, fm)
    r2 = [
        remote(v_out.at[pl.ds(peer_spots[d] * 16, 16)], r2_in.at[d], peers[d]) for d in range(7)
    ]
    ft = dot(dot(g_inv, g_coup), g_top)
    ft_t = ft.T
    root_out[...] = r_coup + dot(ft_t, dot(g_proj, g_top))
    to_root = [remote(root_out, root_in.at[d], ring[d]) for d in range(3)]
    pump(2)
    block_part = dot(block_rhs, p_inv)

    def again(c, carry):
        here = pl.ds(pl.multiple_of(c * HALF, HALF), HALF)
        resid[:, here] = resid[:, here] - stacked(pairs.at[0], sol[:, here])
        return carry

    lax.fori_loop(0, 2, again, 0)

    arrived(*r2)
    few_rows = pl.ds(pl.multiple_of(node * 16, 16), 16)
    group_rhs = v_out[few_rows]
    for d in range(7):
        group_rhs = group_rhs + r2_in[d]
    u_out[...] = dot(group_rhs, ft)
    r3 = [remote(u_out, r3_in.at[d], ring[d]) for d in range(3)]
    pump(2)
    group_part = dot(group_rhs, g_inv)

    arrived(*to_root)
    r_inv = spd_inverse(root_out[...] + root_in[0] + root_in[1] + root_in[2])
    down = dot(r_inv, ft_t)

    arrived(*r3)
    root_rhs = u_out[...] + r3_in[0] + r3_in[1] + r3_in[2]
    gout[few_rows] = group_part + dot(root_rhs, down)
    r4 = [remote(gout.at[few_rows], gout.at[few_rows], peers[d]) for d in range(7)]
    pump(2)

    def keep(ref, here, value):
        high, low = split(value)
        ref[0, :, here] = high
        ref[1, :, here] = low

    for pair in expand_in:
        arrived(*pair)
    every = pl.ds(0, RANK)
    keep(out_o, every, expand[...])
    keep(cross_o, every, stacked(pairs.at[0], expand[...]))
    for k in range(2):
        keep(cross_o, pl.ds((k + 1) * RANK, RANK), stacked(pairs.at[k + 1], expand_halo[k]))

    def sides(c):
        here = cols(c)
        for pair in halo2_in[c]:
            arrived(*pair)

        def side2(k, carry):
            resid[:, here] = resid[:, here] - stacked(pairs.at[k + 1], halo2[k, :, here])
            return carry

        lax.fori_loop(0, 2, side2, 0)

    sides(0)

    arrived(*r4)
    block_own[...] = block_part + dot(gout[...], mf)
    block_out[wide_rows] = block_own[...]
    r5 = [remote(block_own, block_out.at[wide_rows], mates[d]) for d in range(3)]
    k5 = counter[0]
    ahead = [at(index - j + 4), at(index - j + 127)]
    extra = [
        pltpu.make_async_remote_copy(
            src_ref=block_own,
            dst_ref=block_halo.at[wide_rows],
            send_sem=send_sem.at[k5 + way],
            recv_sem=recv_sem.at[k5 + 2 + j],
            device_id=ahead[way],
            device_id_type=MESH,
        )
        for way in range(2)
    ]
    for copy in extra:
        copy.start()

    sides(1)
    left_store = pltpu.make_async_copy(resid, left_o, store_sem.at[1])
    left_store.start()

    arrived(*r5)
    high, low = split(block_out[...].T)
    for k in range(3):
        node_o[0, pl.ds(k * RANK, RANK)] = high
        node_o[1, pl.ds(k * RANK, RANK)] = low

    def from_halo(k):
        for spot in range(4):
            pltpu.make_async_remote_copy(
                src_ref=block_own,
                dst_ref=block_halo.at[pl.ds(spot * 128, 128)],
                send_sem=send_sem.at[k5],
                recv_sem=recv_sem.at[k5 + 2 + spot],
                device_id=ahead[0],
                device_id_type=MESH,
            ).wait_recv()
        high, low = split(block_halo[...].T)
        node_o[0, pl.ds(k * RANK, RANK)] = high
        node_o[1, pl.ds(k * RANK, RANK)] = low

    @pl.when(j == 0)
    def _():
        from_halo(1)

    @pl.when(j == 3)
    def _():
        from_halo(2)

    for pair in pieces[-2:]:
        for copy in pair:
            copy.wait_send()
    for copy in sent + extra:
        copy.wait_send()
    base_store.wait()
    left_store.wait()


def last_kernel(base_ref, left_ref, out_ref, cross_ref, node_ref, guess_ref, resid_ref):
    def three(left, count):
        return (
            plain(left[0], node_ref[0, :count])
            + plain(left[1], node_ref[0, :count])
            + plain(left[0], node_ref[1, :count])
        )

    guess_ref[...] = base_ref[...] - three(out_ref, RANK)
    resid_ref[...] = left_ref[...] + three(cross_ref, 3 * RANK)


def tree(*args):
    any_spec = pl.BlockSpec(memory_space=pl.ANY)
    vmem = pl.BlockSpec(memory_space=pltpu.VMEM)

    def buf(*shape, dtype=F32):
        return pltpu.VMEM(shape, dtype)

    scratch = [
        buf(4, LEAF, LEAF),
        buf(4, 2 * LEAF, LEAF, dtype=BF16),
        buf(LEAF, RHS),
        buf(LEAF, RHS),
        buf(LEAF, RHS),
        buf(LEAF, RHS),
        buf(LEAF, RHS),
        buf(2, LEAF, RHS),
        buf(2, LEAF, RHS),
        buf(LEAF, RANK),
        buf(RANK, RANK),
        buf(LEAF, RANK),
        buf(2, LEAF, RANK),
        buf(2 * RANK, LEAF, dtype=BF16),
        buf(5, RANK, RANK),
        buf(RANK, RANK),
        buf(RANK, RANK),
        buf(RANK, RANK),
        buf(5, 64, RANK),
        buf(5, 64, RANK),
        buf(2, 64, RANK),
        buf(2, RANK, RANK),
        buf(3, 3, 16, RANK),
        buf(3, 16, RANK),
        buf(3, 3, 16, RANK),
        buf(4, RANK, RANK),
        buf(RANK, RANK),
        buf(3, 64, RANK),
        buf(64, RANK),
        buf(64, RANK),
        buf(RANK, RANK),
        buf(3, RANK, RANK),
        buf(RHS, RANK),
        buf(3, RANK, RANK),
        buf(RANK, RANK),
        buf(7, 16, RANK),
        buf(16, RANK),
        buf(3, 16, RANK),
        buf(RANK, RANK),
        buf(RANK, RANK),
        buf(RHS, RANK),
        buf(RHS, RANK),
        pltpu.SemaphoreType.DMA((12,)),
        pltpu.SemaphoreType.DMA((2,)),
        pltpu.SemaphoreType.DMA((96,)),
        pltpu.SemaphoreType.DMA((96,)),
    ]
    base, left, out, cross, node = pl.pallas_call(
        tree_kernel,
        out_shape=[
            jax.ShapeDtypeStruct((LEAF, RHS), F32),
            jax.ShapeDtypeStruct((LEAF, RHS), F32),
            jax.ShapeDtypeStruct((2, LEAF, RANK), BF16),
            jax.ShapeDtypeStruct((2, LEAF, 3 * RANK), BF16),
            jax.ShapeDtypeStruct((2, 3 * RANK, RHS), BF16),
        ],
        in_specs=[any_spec] * 11,
        out_specs=[any_spec, any_spec, vmem, vmem, vmem],
        scratch_shapes=scratch,
        compiler_params=pltpu.CompilerParams(
            collective_id=0, has_side_effects=True, vmem_limit_bytes=56 * 2**20
        ),
    )(*args)
    block = 128
    return pl.pallas_call(
        last_kernel,
        grid=(LEAF // block,),
        in_specs=[
            pl.BlockSpec((block, RHS), lambda i: (i, 0)),
            pl.BlockSpec((block, RHS), lambda i: (i, 0)),
            pl.BlockSpec((2, block, RANK), lambda i: (0, i, 0)),
            pl.BlockSpec((2, block, 3 * RANK), lambda i: (0, i, 0)),
            pl.BlockSpec((2, 3 * RANK, RHS), lambda i: (0, 0, 0)),
        ],
        out_specs=[
            pl.BlockSpec((block, RHS), lambda i: (i, 0)),
            pl.BlockSpec((block, RHS), lambda i: (i, 0)),
        ],
        out_shape=[jax.ShapeDtypeStruct((LEAF, RHS), F32)] * 2,
    )(base, left, out, cross, node)


def body(
    right_side,
    guess,
    near_diag,
    near_lower,
    near_upper,
    leaf_inverse,
    leaf_basis,
    leaf_transfer,
    mid_share,
    top_share,
    coupling_share,
):
    new_guess, new_residual = tree(
        right_side,
        guess,
        near_diag[0],
        near_lower[0],
        near_upper[0],
        leaf_inverse[0],
        leaf_basis[0],
        leaf_transfer[0],
        mid_share[0],
        top_share[0],
        coupling_share[0],
    )
    return (new_guess, new_residual)


def solution(mesh):
    field = P(("grp", "leaf"), None)
    block = P(("grp", "leaf"), None, None)
    shares = P(("grp", "leaf"), None, None, None)
    in_specs = (field, field) + (block,) * 8 + (shares,)
    return jax.shard_map(
        body, mesh=mesh, in_specs=in_specs, out_specs=(field, field), check_vma=False
    )
```

```python
import jax
import jax.numpy as jnp
from jax import lax
from jax.experimental import pallas as pl
from jax.experimental.pallas import tpu as pltpu
from jax.sharding import PartitionSpec as P

MESH = pl.DeviceIdType.MESH
F32 = jnp.float32
BF16 = jnp.bfloat16
LEAF, RANK, RHS = 768, 128, 512
HALF = RHS // 2


def dot(left, right, over=(1, 0)):
    return lax.dot_general(
        left,
        right,
        (((over[0],), (over[1],)), ((), ())),
        precision=lax.Precision.HIGHEST,
        preferred_element_type=F32,
    )


def split(value):
    high = value.astype(BF16)
    return high, (value - high.astype(F32)).astype(BF16)


def plain(left, right, over=(1, 0)):
    return lax.dot_general(
        left, right, (((over[0],), (over[1],)), ((), ())), preferred_element_type=F32
    )


def stacked(pair_ref, value):
    count = pair_ref.shape[0] // 2
    high, low = split(value)
    both = plain(pair_ref[...], high)
    return both[:count] + both[count:] + plain(pair_ref[:count], low)


def spd_inverse(matrix):
    lane = lax.broadcasted_iota(jnp.int32, (8, 128), 1)
    sub = lax.broadcasted_iota(jnp.int32, (8, 128), 0)

    def total(t):
        return ((t[0] + t[1]) + (t[2] + t[3])) + ((t[4] + t[5]) + (t[6] + t[7]))

    def panel(rows, s):
        at = 8 * s
        head = (lane >= at) & (lane < at + 8)
        p = rows[s]
        sc = {}
        for k in range(8):
            col = jnp.broadcast_to(p[:, at + k : at + k + 1], (8, 128))
            for i in range(k + 1):
                sc[i, k] = jnp.broadcast_to(col[i : i + 1, :], (8, 128))

        def get(i, k):
            return sc[min(i, k), max(i, k)]

        for q in range(0, 8, 2):
            aa, bb, cc = sc[q, q], sc[q, q + 1], sc[q + 1, q + 1]
            det = aa * cc - bb * bb
            inv = pl.reciprocal(det, approx=True)
            inv = inv * (2.0 - det * inv)
            inv = inv * (2.0 - det * inv)
            ia, ib, ic = cc * inv, -bb * inv, aa * inv
            others = [i for i in range(8) if i not in (q, q + 1)]
            p0 = {i: get(i, q) for i in others}
            p1 = {i: get(i, q + 1) for i in others}
            q0 = {i: ia * p0[i] + ib * p1[i] for i in others}
            q1 = {i: ib * p0[i] + ic * p1[i] for i in others}
            for i in others:
                for k in others:
                    if i <= k:
                        sc[i, k] = sc[i, k] - (p0[i] * q0[k] + p1[i] * q1[k])
            for i in others:
                sc[min(i, q), max(i, q)] = q0[i]
                sc[min(i, q + 1), max(i, q + 1)] = q1[i]
            sc[q, q], sc[q, q + 1], sc[q + 1, q + 1] = -ia, -ib, -ic
        pm = jnp.where(head, jnp.where(lane == sub + at, -1.0, 0.0), p)
        pb = [jnp.broadcast_to(pm[m : m + 1, :], (8, 128)) for m in range(8)]
        nq = [total([get(k, m) * pb[m] for m in range(8)]) for k in range(8)]
        out = list(rows)
        for i in [(s + 1 + i) % 16 for i in range(15)]:
            r = rows[i]
            terms = [
                jnp.broadcast_to(r[:, at + k : at + k + 1], (8, 128)) * nq[k] for k in range(8)
            ]
            out[i] = jnp.where(head, 0.0, r) + total(terms)
        t = nq[7]
        for k in range(7):
            t = jnp.where(sub == k, nq[k], t)
        out[s] = -t
        return out

    def step(_, rows):
        rows = list(rows)
        for s in range(4):
            rows = panel(rows, s)
        rows = [pltpu.roll(r, 96, 1) for r in rows]
        return tuple(rows[4:] + rows[:4])

    rows = tuple(matrix[8 * i : 8 * i + 8, :] for i in range(16))
    rows = lax.fori_loop(0, 4, step, rows)
    return -jnp.concatenate(rows, 0)


def tree_kernel(
    right_h,
    guess_h,
    diag_h,
    lower_h,
    upper_h,
    inverse_h,
    basis_h,
    trans_h,
    mid_h,
    top_h,
    coup_h,
    base_o,
    left_o,
    out_o,
    cross_o,
    node_o,
    wide,
    pairs,
    right,
    guess,
    resid,
    sol,
    base,
    halo,
    halo2,
    basis,
    trans,
    expand,
    expand_halo,
    project,
    share,
    proj,
    proj_in,
    proj_z,
    chip,
    chip_in,
    pair_in,
    node_m,
    sx_in,
    sx_out,
    sz_in,
    group_m,
    q_out,
    xq_in,
    zq_out,
    zq_in,
    root_out,
    root_in,
    reduced,
    reduced_in,
    r1_in,
    kept,
    block_rhs,
    v_out,
    r2_in,
    u_out,
    r3_in,
    part,
    gout,
    block_own,
    block_out,
    block_halo,
    load_sem,
    store_sem,
    send_sem,
    recv_sem,
):
    y = lax.axis_index("grp")
    l = lax.axis_index("leaf")
    core = l % 2
    j = l % 4
    z = (l // 2) % 4
    zp = z % 2
    x = l // 8
    node = l // 4
    first = l - j
    index = y * 32 + l

    def at(place):
        place = place % 128
        return (place // 32, place % 32)

    def on(which):
        return pl.when(core == which)

    twin = (y, l + 1 - 2 * core)
    up = at(index + 1)
    down_chip = at(index + 126)
    up_chip = at(index + 2)
    before = at(index + 127)
    mate_z = (y, first + core + 2 - 2 * zp)
    mate_z1 = (y, first + 3 - 2 * zp)
    x_spots = [(x + d) % 4 for d in (1, 2, 3)]
    cross = [(y, (l + 8 * d) % 32) for d in (1, 2, 3)]
    line = [(y, x * 8 + ((z + d) % 4) * 2 + core) for d in (1, 2, 3)]
    peers = [(y, (l + 4 * d) % 32) for d in range(1, 8)]
    peer_spots = [(node + d) % 8 for d in range(1, 8)]
    ring = [((y + d) % 4, l) for d in (1, 2, 3)]
    ahead = [at(index - j + 4), at(index - j + 127)]

    counter = [0]
    sent = {0: [], 1: []}

    def message(src, dst, device, which):
        k = counter[0]
        counter[0] += 1
        copy = pltpu.make_async_remote_copy(
            src_ref=src,
            dst_ref=dst,
            send_sem=send_sem.at[k],
            recv_sem=recv_sem.at[k],
            device_id=device,
            device_id_type=MESH,
        )
        sent[which].append(copy)
        return copy

    def begin(*copies):
        for copy in copies:
            copy.start()

    def arrived(*copies):
        for copy in copies:
            copy.wait_recv()

    local = []

    def load(src, dst):
        copy = pltpu.make_async_copy(src, dst, load_sem.at[len(local)])
        copy.start()
        local.append(copy)
        return copy

    load_inverse = load(inverse_h, wide.at[3])
    load_basis = load(basis_h, basis)
    load_trans = load(trans_h, trans)
    load_share = [
        load(coup_h.at[0], share.at[0]),
        load(mid_h, share.at[1]),
        load(coup_h.at[pl.ds(1, 2)], share.at[pl.ds(2, 2)]),
        load(top_h, share.at[4]),
    ]
    load_guess = load(guess_h, guess)
    load_diag = load(diag_h, wide.at[0])
    load_right = load(right_h, right)
    load_lower = load(lower_h, wide.at[1])
    load_upper = load(upper_h, wide.at[2])

    barrier = pltpu.get_barrier_semaphore()

    def hello(device):
        pl.semaphore_signal(barrier, inc=1, device_id=device, device_id_type=MESH)

    @on(1)
    def _():
        for device in (twin, up_chip, (y, first + 2 - 2 * zp)):
            hello(device)

    @on(0)
    def _():
        for device in [twin, before] + line + cross + peers + ring:
            hello(device)

    @pl.when(j == 0)
    def _():
        hello(at(index + 124))
        hello(at(index + 126))

    @pl.when(j == 3)
    def _():
        hello(at(index + 1))
        hello(at(index + 3))

    @on(1)
    def _():
        pl.semaphore_wait(barrier, 3)

    @on(0)
    def _():
        pl.semaphore_wait(barrier, 20)

    def cols(c):
        return pl.ds(c * HALF, HALF)

    class Part:
        def __init__(self, src, dst, place):
            low, high = dst.at[(0,) + place], dst.at[(1,) + place]
            self.low = message(src.at[place], low, twin, 0)
            k = counter[0]
            counter[0] += 3

            def one(src, dst, device, send, recv):
                copy = pltpu.make_async_remote_copy(
                    src_ref=src,
                    dst_ref=dst,
                    send_sem=send_sem.at[send],
                    recv_sem=recv_sem.at[recv],
                    device_id=device,
                    device_id_type=MESH,
                )
                sent[1].append(copy)
                return copy

            self.high = one(src.at[place], high, twin, k, k)
            self.up = one(src.at[place], low, up, k + 1, k - 1)
            self.down = one(low, high, down_chip, k + 2, k)

    def quarters(src, dst, c):
        return [Part(src, dst, (pl.ds(192 * q, 192), cols(c))) for q in range(4)]

    halo_in = quarters(guess_h, halo, 0) + quarters(guess_h, halo, 1)
    whole = pl.ds(0, LEAF)
    expand_in = Part(expand, expand_halo, (whole, pl.ds(0, RANK)))
    halo2_in = [Part(sol, halo2, (whole, cols(c))) for c in range(2)]

    e1 = message(share, chip_in, twin, 1)
    e_core = message(proj, proj_in, twin, 1)

    @on(1)
    def _():
        begin(halo_in[0].up, halo_in[0].high)
        for copy in load_share:
            copy.wait()
        begin(e1, halo_in[1].up, halo_in[1].high)
        for k in range(2):
            arrived(halo_in[k].low)
            begin(halo_in[k].down)

    @on(0)
    def _():
        for piece in halo_in:
            begin(piece.low)

    load_inverse.wait()
    load_basis.wait()
    load_trans.wait()
    basis_t = basis[...].T
    trans_t = trans[...].T
    weighted = dot(wide[3], basis[...])
    proj[...] = dot(trans_t, dot(dot(basis_t, weighted), trans[...]))

    @on(1)
    def _():
        begin(e_core)
        for piece in halo_in[2:]:
            begin(piece.up, piece.high)
            arrived(piece.low)
            begin(piece.down)

    x_rows = pl.ds(pl.multiple_of(x * 32, 32), 32)
    e_pair = message(chip.at[pl.ds(0, 2)], pair_in, mate_z, 0)
    sx = [
        message(chip.at[pl.ds(2, 3), pl.ds(x_spots[d] * 32, 32)], sx_in.at[d], cross[d], 0)
        for d in range(3)
    ]
    sz = [message(sx_out, sz_in.at[d], line[d], 0) for d in range(3)]
    sx2 = [
        message(
            group_m.at[pl.ds(0, 3), x_rows], group_m.at[pl.ds(0, 3), x_rows], cross[d], 0
        )
        for d in range(3)
    ]
    e_z = message(proj, proj_z, mate_z, 0)

    @on(0)
    def _():
        for copy in load_share:
            copy.wait()
        arrived(e1)
        chip[...] = share[...] + chip_in[...]
        begin(e_pair, *sx)
        arrived(e_core)
        proj[...] = proj[...] + proj_in[...]
        begin(e_z)

    expand[...] = dot(weighted, trans[...])
    high, low = split(dot(trans_t, basis_t))
    project[pl.ds(0, RANK)] = high
    project[pl.ds(RANK, RANK)] = low

    def divide(m, scale=None):
        value = wide[m]
        if scale is not None:
            value = value * scale
        high, low = split(value)
        pairs[m, pl.ds(0, LEAF)] = high
        pairs[m, pl.ds(LEAF, LEAF)] = low

    load_guess.wait()
    load_diag.wait()
    load_right.wait()
    divide(0)

    def own(c, carry):
        here = pl.ds(pl.multiple_of(c * HALF, HALF), HALF)
        resid[:, here] = right[:, here] - stacked(pairs.at[0], guess[:, here])
        return carry

    lax.fori_loop(0, 2, own, 0)

    xq = [message(q_out, xq_in.at[d], cross[d], 0) for d in range(3)]

    @on(0)
    def _():
        begin(expand_in.low)
        arrived(*sx)
        sx_out[...] = chip[2:5, x_rows] + sx_in[0] + sx_in[1] + sx_in[2]
        begin(*sz)
        arrived(e_pair)
        node_m[...] = chip[0:2] + pair_in[...]
        arrived(e_z)
        p_proj, p_coup, p_mid = proj[...] + proj_z[...], node_m[0], node_m[1]
        p_inv = spd_inverse(p_proj + p_coup)
        fm = dot(dot(p_inv, p_coup), p_mid)
        mf = fm.T
        q_out[...] = dot(mf, dot(p_proj, p_mid))
        begin(*xq)
        kept[0] = p_inv
        kept[1] = fm
        kept[2] = mf
        arrived(*sz)
        group_m[pl.ds(0, 3), x_rows] = sx_out[...] + sz_in[0] + sz_in[1] + sz_in[2]
        begin(*sx2)

    load_lower.wait()
    load_upper.wait()
    divide(1, jnp.where(index == 0, 0.0, 1.0))
    divide(2, jnp.where(index == 127, 0.0, 1.0))
    divide(3)

    def leaf_chunk(c):
        here = cols(c)
        for piece in halo_in[4 * c : 4 * c + 4]:
            arrived(piece.high)

        @on(0)
        def _():
            for piece in halo_in[4 * c : 4 * c + 4]:
                arrived(piece.low)

        def side(k, carry):
            resid[:, here] = resid[:, here] - stacked(pairs.at[k + 1], halo[k, :, here])
            return carry

        lax.fori_loop(0, 2, side, 0)
        sol[:, here] = stacked(pairs.at[3], resid[:, here])

    def reduce_chunk(c):
        here = cols(c)
        reduced[here, :] = stacked(project, sol[:, here]).T

    to_core = [message(reduced.at[cols(c)], reduced_in.at[cols(c)], twin, 1) for c in range(2)]

    leaf_chunk(0)
    reduce_chunk(0)

    @on(1)
    def _():
        begin(to_core[0], expand_in.up, expand_in.high)
        arrived(expand_in.low)
        begin(expand_in.down, halo2_in[0].high)

    zq = message(zq_out, zq_in, line[1], 0)

    @on(0)
    def _():
        begin(halo2_in[0].low)
        arrived(*xq)
        zq_out[...] = q_out[...] + xq_in[0] + xq_in[1] + xq_in[2]
        begin(zq)

    base[:, cols(0)] = guess[:, cols(0)] + sol[:, cols(0)]
    leaf_chunk(1)
    reduce_chunk(1)

    @on(1)
    def _():
        begin(to_core[1], halo2_in[0].up)
        arrived(halo2_in[0].low)
        begin(halo2_in[0].down, halo2_in[1].high, halo2_in[1].up)
        arrived(halo2_in[1].low)
        begin(halo2_in[1].down)

    half = pl.ds(pl.multiple_of(zp * 256, 256), 256)
    other = pl.ds(pl.multiple_of(256 - zp * 256, 256), 256)
    r1 = message(reduced.at[other], r1_in, mate_z, 0)
    to_root = [message(root_out, root_in.at[d], ring[d], 0) for d in range(3)]
    r2 = [
        message(v_out.at[pl.ds(peer_spots[d] * 32, 32)], r2_in.at[d], peers[d], 0)
        for d in range(7)
    ]

    @on(0)
    def _():
        begin(halo2_in[1].low)
        arrived(*to_core)
        reduced[...] = reduced[...] + reduced_in[...]
        begin(r1)

    base[:, cols(1)] = guess[:, cols(1)] + sol[:, cols(1)]
    base_store = pltpu.make_async_copy(base, base_o, store_sem.at[0])
    base_store.start()

    @on(0)
    def _():
        arrived(*sx2)
        arrived(zq)
        g_coup, r_coup, g_top = group_m[0], group_m[1], group_m[2]
        g_proj = zq_out[...] + zq_in[...]
        g_inv = spd_inverse(g_proj + g_coup)
        arrived(r1)
        block_rhs[...] = reduced[half] + r1_in[...]
        v_out[...] = dot(block_rhs[...], kept[1])
        begin(*r2)
        ft = dot(dot(g_inv, g_coup), g_top)
        ft_t = ft.T
        root_out[...] = r_coup + dot(ft_t, dot(g_proj, g_top))
        begin(*to_root)
        kept[3] = g_inv
        kept[4] = ft
        kept[5] = ft_t

    def again(c, carry):
        here = pl.ds(pl.multiple_of(c * HALF, HALF), HALF)
        resid[:, here] = resid[:, here] - stacked(pairs.at[0], sol[:, here])
        return carry

    lax.fori_loop(0, 2, again, 0)

    few_rows = pl.ds(pl.multiple_of(node * 32, 32), 32)
    r3 = [message(u_out, r3_in.at[d], ring[d], 0) for d in range(3)]
    r4 = [message(gout.at[few_rows], gout.at[few_rows], peers[d], 0) for d in range(7)]

    @on(0)
    def _():
        arrived(*r2)
        group_rhs = v_out[few_rows]
        for d in range(7):
            group_rhs = group_rhs + r2_in[d]
        u_out[...] = dot(group_rhs, kept[4])
        begin(*r3)
        part[...] = dot(group_rhs, kept[3])
        arrived(*to_root)
        r_inv = spd_inverse(root_out[...] + root_in[0] + root_in[1] + root_in[2])
        down = dot(r_inv, kept[5])
        arrived(*r3)
        root_rhs = u_out[...] + r3_in[0] + r3_in[1] + r3_in[2]
        gout[few_rows] = part[...] + dot(root_rhs, down)
        begin(*r4)

    def keep(ref, here, value):
        high, low = split(value)
        ref[0, :, here] = high
        ref[1, :, here] = low

    arrived(expand_in.high)

    @on(0)
    def _():
        arrived(expand_in.low)

    keep(out_o, pl.ds(0, RANK), expand[...])
    keep(cross_o, pl.ds(0, RANK), stacked(pairs.at[0], expand[...]))
    for k in range(2):
        keep(cross_o, pl.ds((k + 1) * RANK, RANK), stacked(pairs.at[k + 1], expand_halo[k]))

    def sides(c):
        here = cols(c)
        arrived(halo2_in[c].high)

        @on(0)
        def _():
            arrived(halo2_in[c].low)

        def side2(k, carry):
            resid[:, here] = resid[:, here] - stacked(pairs.at[k + 1], halo2[k, :, here])
            return carry

        lax.fori_loop(0, 2, side2, 0)

    sides(0)

    r5 = message(block_own, block_out.at[half], mate_z, 0)
    r5_twin = message(block_own, block_out.at[half], twin, 0)
    r5_far = message(block_own, block_out.at[half], mate_z1, 0)
    k5 = counter[0]
    extra = [
        pltpu.make_async_remote_copy(
            src_ref=block_own,
            dst_ref=block_halo.at[half],
            send_sem=send_sem.at[k5 + way],
            recv_sem=recv_sem.at[k5 + zp],
            device_id=ahead[way],
            device_id_type=MESH,
        )
        for way in range(2)
    ]

    @on(0)
    def _():
        arrived(*r4)
        block_own[...] = dot(block_rhs[...], kept[0]) + dot(gout[...], kept[2])
        begin(r5, r5_far, r5_twin, *extra)
        block_out[half] = block_own[...]

    sides(1)
    left_store = pltpu.make_async_copy(resid, left_o, store_sem.at[1])
    left_store.start()

    @on(0)
    def _():
        arrived(r5)

    @on(1)
    def _():
        arrived(r5_twin, r5_far)

    high, low = split(block_out[...].T)
    for k in range(3):
        node_o[0, pl.ds(k * RANK, RANK)] = high
        node_o[1, pl.ds(k * RANK, RANK)] = low

    def from_halo(k):
        for spot in range(2):
            pltpu.make_async_remote_copy(
                src_ref=block_own,
                dst_ref=block_halo.at[pl.ds(spot * 256, 256)],
                send_sem=send_sem.at[k5],
                recv_sem=recv_sem.at[k5 + spot],
                device_id=ahead[0],
                device_id_type=MESH,
            ).wait_recv()
        high, low = split(block_halo[...].T)
        node_o[0, pl.ds(k * RANK, RANK)] = high
        node_o[1, pl.ds(k * RANK, RANK)] = low

    @pl.when(j == 0)
    def _():
        from_halo(1)

    @pl.when(j == 3)
    def _():
        from_halo(2)

    for which in range(2):

        @on(which)
        def _():
            for copy in sent[which]:
                copy.wait_send()
            if which == 0:
                for copy in extra:
                    copy.wait_send()

    base_store.wait()
    left_store.wait()


def last_kernel(base_ref, left_ref, out_ref, cross_ref, node_ref, guess_ref, resid_ref):
    def three(left, count):
        return (
            plain(left[0], node_ref[0, :count])
            + plain(left[1], node_ref[0, :count])
            + plain(left[0], node_ref[1, :count])
        )

    guess_ref[...] = base_ref[...] - three(out_ref, RANK)
    resid_ref[...] = left_ref[...] + three(cross_ref, 3 * RANK)


def tree(*args):
    any_spec = pl.BlockSpec(memory_space=pl.ANY)
    vmem = pl.BlockSpec(memory_space=pltpu.VMEM)

    def buf(*shape, dtype=F32):
        return pltpu.VMEM(shape, dtype)

    scratch = [
        buf(4, LEAF, LEAF),
        buf(4, 2 * LEAF, LEAF, dtype=BF16),
        buf(LEAF, RHS),
        buf(LEAF, RHS),
        buf(LEAF, RHS),
        buf(LEAF, RHS),
        buf(LEAF, RHS),
        buf(2, LEAF, RHS),
        buf(2, LEAF, RHS),
        buf(LEAF, RANK),
        buf(RANK, RANK),
        buf(LEAF, RANK),
        buf(2, LEAF, RANK),
        buf(2 * RANK, LEAF, dtype=BF16),
        buf(5, RANK, RANK),
        buf(RANK, RANK),
        buf(RANK, RANK),
        buf(RANK, RANK),
        buf(5, RANK, RANK),
        buf(5, RANK, RANK),
        buf(2, RANK, RANK),
        buf(2, RANK, RANK),
        buf(3, 3, 32, RANK),
        buf(3, 32, RANK),
        buf(3, 3, 32, RANK),
        buf(3, RANK, RANK),
        buf(RANK, RANK),
        buf(3, RANK, RANK),
        buf(RANK, RANK),
        buf(RANK, RANK),
        buf(RANK, RANK),
        buf(3, RANK, RANK),
        buf(RHS, RANK),
        buf(RHS, RANK),
        buf(HALF, RANK),
        buf(6, RANK, RANK),
        buf(HALF, RANK),
        buf(HALF, RANK),
        buf(7, 32, RANK),
        buf(32, RANK),
        buf(3, 32, RANK),
        buf(32, RANK),
        buf(HALF, RANK),
        buf(HALF, RANK),
        buf(RHS, RANK),
        buf(RHS, RANK),
        pltpu.SemaphoreType.DMA((12,)),
        pltpu.SemaphoreType.DMA((2,)),
        pltpu.SemaphoreType.DMA((112,)),
        pltpu.SemaphoreType.DMA((112,)),
    ]
    base, left, out, cross, node = pl.pallas_call(
        tree_kernel,
        out_shape=[
            jax.ShapeDtypeStruct((LEAF, RHS), F32),
            jax.ShapeDtypeStruct((LEAF, RHS), F32),
            jax.ShapeDtypeStruct((2, LEAF, RANK), BF16),
            jax.ShapeDtypeStruct((2, LEAF, 3 * RANK), BF16),
            jax.ShapeDtypeStruct((2, 3 * RANK, RHS), BF16),
        ],
        in_specs=[any_spec] * 11,
        out_specs=[any_spec, any_spec, vmem, vmem, vmem],
        scratch_shapes=scratch,
        compiler_params=pltpu.CompilerParams(
            collective_id=0, has_side_effects=True, vmem_limit_bytes=56 * 2**20
        ),
    )(*args)
    block = 128
    return pl.pallas_call(
        last_kernel,
        grid=(LEAF // block,),
        in_specs=[
            pl.BlockSpec((block, RHS), lambda i: (i, 0)),
            pl.BlockSpec((block, RHS), lambda i: (i, 0)),
            pl.BlockSpec((2, block, RANK), lambda i: (0, i, 0)),
            pl.BlockSpec((2, block, 3 * RANK), lambda i: (0, i, 0)),
            pl.BlockSpec((2, 3 * RANK, RHS), lambda i: (0, 0, 0)),
        ],
        out_specs=[
            pl.BlockSpec((block, RHS), lambda i: (i, 0)),
            pl.BlockSpec((block, RHS), lambda i: (i, 0)),
        ],
        out_shape=[jax.ShapeDtypeStruct((LEAF, RHS), F32)] * 2,
    )(base, left, out, cross, node)


def body(
    right_side,
    guess,
    near_diag,
    near_lower,
    near_upper,
    leaf_inverse,
    leaf_basis,
    leaf_transfer,
    mid_share,
    top_share,
    coupling_share,
):
    new_guess, new_residual = tree(
        right_side,
        guess,
        near_diag[0],
        near_lower[0],
        near_upper[0],
        leaf_inverse[0],
        leaf_basis[0],
        leaf_transfer[0],
        mid_share[0],
        top_share[0],
        coupling_share[0],
    )
    return (new_guess, new_residual)


def solution(mesh):
    field = P(("grp", "leaf"), None)
    block = P(("grp", "leaf"), None, None)
    shares = P(("grp", "leaf"), None, None, None)
    in_specs = (field, field) + (block,) * 8 + (shares,)
    return jax.shard_map(
        body, mesh=mesh, in_specs=in_specs, out_specs=(field, field), check_vma=False
    )
```

```python
import jax
import jax.numpy as jnp
from jax import lax
from jax.experimental import pallas as pl
from jax.experimental.pallas import tpu as pltpu
from jax.sharding import PartitionSpec as P

MESH = pl.DeviceIdType.MESH
F32 = jnp.float32
BF16 = jnp.bfloat16
LEAF, RANK, RHS = 768, 128, 512
HALF = RHS // 2


def dot(left, right, over=(1, 0)):
    return lax.dot_general(
        left,
        right,
        (((over[0],), (over[1],)), ((), ())),
        precision=lax.Precision.HIGHEST,
        preferred_element_type=F32,
    )


def split(value):
    high = value.astype(BF16)
    return high, (value - high.astype(F32)).astype(BF16)


def plain(left, right, over=(1, 0)):
    return lax.dot_general(
        left, right, (((over[0],), (over[1],)), ((), ())), preferred_element_type=F32
    )


def stacked(pair_ref, value):
    count = pair_ref.shape[0] // 2
    high, low = split(value)
    both = plain(pair_ref[...], high)
    return both[:count] + both[count:] + plain(pair_ref[:count], low)


def spd_inverse(matrix):
    lane = lax.broadcasted_iota(jnp.int32, (8, 128), 1)
    sub = lax.broadcasted_iota(jnp.int32, (8, 128), 0)

    def total(t):
        return ((t[0] + t[1]) + (t[2] + t[3])) + ((t[4] + t[5]) + (t[6] + t[7]))

    def panel(rows, s):
        at = 8 * s
        head = (lane >= at) & (lane < at + 8)
        p = rows[s]
        sc = {}
        for k in range(8):
            col = jnp.broadcast_to(p[:, at + k : at + k + 1], (8, 128))
            for i in range(k + 1):
                sc[i, k] = jnp.broadcast_to(col[i : i + 1, :], (8, 128))

        def get(i, k):
            return sc[min(i, k), max(i, k)]

        for q in range(0, 8, 2):
            aa, bb, cc = sc[q, q], sc[q, q + 1], sc[q + 1, q + 1]
            det = aa * cc - bb * bb
            inv = pl.reciprocal(det, approx=True)
            inv = inv * (2.0 - det * inv)
            inv = inv * (2.0 - det * inv)
            ia, ib, ic = cc * inv, -bb * inv, aa * inv
            others = [i for i in range(8) if i not in (q, q + 1)]
            p0 = {i: get(i, q) for i in others}
            p1 = {i: get(i, q + 1) for i in others}
            q0 = {i: ia * p0[i] + ib * p1[i] for i in others}
            q1 = {i: ib * p0[i] + ic * p1[i] for i in others}
            for i in others:
                for k in others:
                    if i <= k:
                        sc[i, k] = sc[i, k] - (p0[i] * q0[k] + p1[i] * q1[k])
            for i in others:
                sc[min(i, q), max(i, q)] = q0[i]
                sc[min(i, q + 1), max(i, q + 1)] = q1[i]
            sc[q, q], sc[q, q + 1], sc[q + 1, q + 1] = -ia, -ib, -ic
        pm = jnp.where(head, jnp.where(lane == sub + at, -1.0, 0.0), p)
        pb = [jnp.broadcast_to(pm[m : m + 1, :], (8, 128)) for m in range(8)]
        nq = [total([get(k, m) * pb[m] for m in range(8)]) for k in range(8)]
        out = list(rows)
        for i in [(s + 1 + i) % 16 for i in range(15)]:
            r = rows[i]
            terms = [
                jnp.broadcast_to(r[:, at + k : at + k + 1], (8, 128)) * nq[k] for k in range(8)
            ]
            out[i] = jnp.where(head, 0.0, r) + total(terms)
        t = nq[7]
        for k in range(7):
            t = jnp.where(sub == k, nq[k], t)
        out[s] = -t
        return out

    def step(_, rows):
        rows = list(rows)
        for s in range(4):
            rows = panel(rows, s)
        rows = [pltpu.roll(r, 96, 1) for r in rows]
        return tuple(rows[4:] + rows[:4])

    rows = tuple(matrix[8 * i : 8 * i + 8, :] for i in range(16))
    rows = lax.fori_loop(0, 4, step, rows)
    return -jnp.concatenate(rows, 0)


def tree_kernel(
    right_h,
    guess_h,
    diag_h,
    lower_h,
    upper_h,
    inverse_h,
    basis_h,
    trans_h,
    mid_h,
    top_h,
    coup_h,
    base_o,
    left_o,
    out_o,
    cross_o,
    node_o,
    wide,
    pairs,
    right,
    guess,
    resid,
    sol,
    base,
    halo,
    halo2,
    basis,
    trans,
    expand,
    expand_halo,
    project,
    share,
    proj,
    proj_in,
    proj_z,
    chip,
    chip_in,
    pair_in,
    node_m,
    sx_in,
    sx_out,
    sz_in,
    group_m,
    q_out,
    xq_in,
    zq_out,
    zq_in,
    root_out,
    root_in,
    reduced,
    reduced_in,
    r1_in,
    kept,
    block_rhs,
    v_out,
    r2_in,
    u_out,
    r3_in,
    part,
    gout,
    block_own,
    block_out,
    block_halo,
    load_sem,
    store_sem,
    send_sem,
    recv_sem,
):
    y = lax.axis_index("grp")
    l = lax.axis_index("leaf")
    core = l % 2
    j = l % 4
    z = (l // 2) % 4
    zp = z % 2
    x = l // 8
    node = l // 4
    first = l - j
    index = y * 32 + l

    def at(place):
        place = place % 128
        return (place // 32, place % 32)

    def on(which):
        return pl.when(core == which)

    twin = (y, l + 1 - 2 * core)
    up = at(index + 1)
    down_chip = at(index + 126)
    up_chip = at(index + 2)
    before = at(index + 127)
    mate_z = (y, first + core + 2 - 2 * zp)
    mate_z1 = (y, first + 3 - 2 * zp)
    x_spots = [(x + d) % 4 for d in (1, 2, 3)]
    cross = [(y, (l + 8 * d) % 32) for d in (1, 2, 3)]
    line = [(y, x * 8 + ((z + d) % 4) * 2 + core) for d in (1, 2, 3)]
    peers = [(y, (l + 4 * d) % 32) for d in range(1, 8)]
    peer_spots = [(node + d) % 8 for d in range(1, 8)]
    ring = [((y + d) % 4, l) for d in (1, 2, 3)]
    ahead = [at(index - j + 4), at(index - j + 127)]

    counter = [0]
    sent = {0: [], 1: []}

    def message(src, dst, device, which):
        k = counter[0]
        counter[0] += 1
        copy = pltpu.make_async_remote_copy(
            src_ref=src,
            dst_ref=dst,
            send_sem=send_sem.at[k],
            recv_sem=recv_sem.at[k],
            device_id=device,
            device_id_type=MESH,
        )
        sent[which].append(copy)
        return copy

    def begin(*copies):
        for copy in copies:
            copy.start()

    def arrived(*copies):
        for copy in copies:
            copy.wait_recv()

    local = []

    def load(src, dst):
        copy = pltpu.make_async_copy(src, dst, load_sem.at[len(local)])
        copy.start()
        local.append(copy)
        return copy

    load_inverse = load(inverse_h, wide.at[3])
    load_basis = load(basis_h, basis)
    load_trans = load(trans_h, trans)
    load_share = [
        load(coup_h.at[0], share.at[0]),
        load(mid_h, share.at[1]),
        load(coup_h.at[pl.ds(1, 2)], share.at[pl.ds(2, 2)]),
        load(top_h, share.at[4]),
    ]
    load_guess = load(guess_h, guess)
    load_diag = load(diag_h, wide.at[0])
    load_right = load(right_h, right)
    load_lower = load(lower_h, wide.at[1])
    load_upper = load(upper_h, wide.at[2])

    barrier = pltpu.get_barrier_semaphore()

    def hello(device):
        pl.semaphore_signal(barrier, inc=1, device_id=device, device_id_type=MESH)

    @on(1)
    def _():
        for device in (twin, up_chip, (y, first + 2 - 2 * zp)):
            hello(device)

    @on(0)
    def _():
        for device in [twin, before] + line + cross + peers + ring:
            hello(device)

    @pl.when(j == 0)
    def _():
        hello(at(index + 124))
        hello(at(index + 126))

    @pl.when(j == 3)
    def _():
        hello(at(index + 1))
        hello(at(index + 3))

    @on(1)
    def _():
        pl.semaphore_wait(barrier, 3)

    @on(0)
    def _():
        pl.semaphore_wait(barrier, 20)

    def cols(c):
        return pl.ds(c * HALF, HALF)

    class Part:
        def __init__(self, src, dst, place):
            low, high = dst.at[(0,) + place], dst.at[(1,) + place]
            self.low = message(src.at[place], low, twin, 0)
            k = counter[0]
            counter[0] += 3

            def one(src, dst, device, send, recv):
                copy = pltpu.make_async_remote_copy(
                    src_ref=src,
                    dst_ref=dst,
                    send_sem=send_sem.at[send],
                    recv_sem=recv_sem.at[recv],
                    device_id=device,
                    device_id_type=MESH,
                )
                sent[1].append(copy)
                return copy

            self.high = one(src.at[place], high, twin, k, k)
            self.up = one(src.at[place], low, up, k + 1, k - 1)
            self.down = one(low, high, down_chip, k + 2, k)

    def quarters(src, dst, c):
        return [Part(src, dst, (pl.ds(192 * q, 192), cols(c))) for q in range(4)]

    halo_in = quarters(guess_h, halo, 0) + quarters(guess_h, halo, 1)
    whole = pl.ds(0, LEAF)
    expand_in = Part(expand, expand_halo, (whole, pl.ds(0, RANK)))
    halo2_in = [Part(sol, halo2, (whole, cols(c))) for c in range(2)]

    e1 = message(share, chip_in, twin, 1)
    e_core = message(proj, proj_in, twin, 1)

    @on(1)
    def _():
        begin(halo_in[0].up, halo_in[0].high)
        for copy in load_share:
            copy.wait()
        begin(e1)
        arrived(halo_in[0].low)
        begin(halo_in[0].down)

    @on(0)
    def _():
        for piece in halo_in:
            begin(piece.low)

    load_inverse.wait()
    load_basis.wait()
    load_trans.wait()
    basis_t = basis[...].T
    trans_t = trans[...].T
    weighted = dot(wide[3], basis[...])
    proj[...] = dot(trans_t, dot(dot(basis_t, weighted), trans[...]))

    @on(1)
    def _():
        begin(e_core)
        for piece in halo_in[1:]:
            begin(piece.up, piece.high)
            arrived(piece.low)
            begin(piece.down)

    x_rows = pl.ds(pl.multiple_of(x * 32, 32), 32)
    e_pair = message(chip.at[pl.ds(0, 2)], pair_in, mate_z, 0)
    sx = [
        message(chip.at[pl.ds(2, 3), pl.ds(x_spots[d] * 32, 32)], sx_in.at[d], cross[d], 0)
        for d in range(3)
    ]
    sz = [message(sx_out, sz_in.at[d], line[d], 0) for d in range(3)]
    sx2 = [
        message(
            group_m.at[pl.ds(0, 3), x_rows], group_m.at[pl.ds(0, 3), x_rows], cross[d], 0
        )
        for d in range(3)
    ]
    e_z = message(proj, proj_z, mate_z, 0)

    @on(0)
    def _():
        for copy in load_share:
            copy.wait()
        arrived(e1)
        chip[...] = share[...] + chip_in[...]
        begin(e_pair, *sx)
        arrived(e_core)
        proj[...] = proj[...] + proj_in[...]
        begin(e_z)

    expand[...] = dot(weighted, trans[...])
    high, low = split(dot(trans_t, basis_t))
    project[pl.ds(0, RANK)] = high
    project[pl.ds(RANK, RANK)] = low

    def divide(m, scale=None):
        value = wide[m]
        if scale is not None:
            value = value * scale
        high, low = split(value)
        pairs[m, pl.ds(0, LEAF)] = high
        pairs[m, pl.ds(LEAF, LEAF)] = low

    load_guess.wait()
    load_diag.wait()
    load_right.wait()
    divide(0)

    def own(c, carry):
        here = pl.ds(pl.multiple_of(c * HALF, HALF), HALF)
        resid[:, here] = right[:, here] - stacked(pairs.at[0], guess[:, here])
        return carry

    lax.fori_loop(0, 2, own, 0)

    xq = [message(q_out, xq_in.at[d], cross[d], 0) for d in range(3)]

    @on(0)
    def _():
        begin(expand_in.low)
        arrived(*sx)
        sx_out[...] = chip[2:5, x_rows] + sx_in[0] + sx_in[1] + sx_in[2]
        begin(*sz)
        arrived(e_pair)
        node_m[...] = chip[0:2] + pair_in[...]
        arrived(e_z)
        p_proj, p_coup, p_mid = proj[...] + proj_z[...], node_m[0], node_m[1]
        p_inv = spd_inverse(p_proj + p_coup)
        fm = dot(dot(p_inv, p_coup), p_mid)
        mf = fm.T
        q_out[...] = dot(mf, dot(p_proj, p_mid))
        begin(*xq)
        kept[0] = p_inv
        kept[1] = fm
        kept[2] = mf
        arrived(*sz)
        group_m[pl.ds(0, 3), x_rows] = sx_out[...] + sz_in[0] + sz_in[1] + sz_in[2]
        begin(*sx2)

    load_lower.wait()
    load_upper.wait()
    divide(1, jnp.where(index == 0, 0.0, 1.0))
    divide(2, jnp.where(index == 127, 0.0, 1.0))
    divide(3)

    def leaf_chunk(c):
        here = cols(c)
        for piece in halo_in[4 * c : 4 * c + 4]:
            arrived(piece.high)

        @on(0)
        def _():
            for piece in halo_in[4 * c : 4 * c + 4]:
                arrived(piece.low)

        def side(k, carry):
            resid[:, here] = resid[:, here] - stacked(pairs.at[k + 1], halo[k, :, here])
            return carry

        lax.fori_loop(0, 2, side, 0)
        sol[:, here] = stacked(pairs.at[3], resid[:, here])

    def reduce_chunk(c):
        here = cols(c)
        reduced[here, :] = stacked(project, sol[:, here]).T

    to_core = [message(reduced.at[cols(c)], reduced_in.at[cols(c)], twin, 1) for c in range(2)]

    leaf_chunk(0)
    reduce_chunk(0)

    @on(1)
    def _():
        begin(to_core[0], expand_in.up, expand_in.high)
        arrived(expand_in.low)
        begin(expand_in.down, halo2_in[0].high)

    zq = message(zq_out, zq_in, line[1], 0)

    @on(0)
    def _():
        begin(halo2_in[0].low)
        arrived(*xq)
        zq_out[...] = q_out[...] + xq_in[0] + xq_in[1] + xq_in[2]
        begin(zq)

    base[:, cols(0)] = guess[:, cols(0)] + sol[:, cols(0)]
    leaf_chunk(1)
    reduce_chunk(1)

    @on(1)
    def _():
        begin(to_core[1], halo2_in[0].up)
        arrived(halo2_in[0].low)
        begin(halo2_in[0].down, halo2_in[1].high, halo2_in[1].up)
        arrived(halo2_in[1].low)
        begin(halo2_in[1].down)

    half = pl.ds(pl.multiple_of(zp * 256, 256), 256)
    other = pl.ds(pl.multiple_of(256 - zp * 256, 256), 256)
    r1 = message(reduced.at[other], r1_in, mate_z, 0)
    to_root = [message(root_out, root_in.at[d], ring[d], 0) for d in range(3)]
    r2 = [
        message(v_out.at[pl.ds(peer_spots[d] * 32, 32)], r2_in.at[d], peers[d], 0)
        for d in range(7)
    ]

    @on(0)
    def _():
        begin(halo2_in[1].low)
        arrived(*to_core)
        reduced[...] = reduced[...] + reduced_in[...]
        begin(r1)

    base[:, cols(1)] = guess[:, cols(1)] + sol[:, cols(1)]
    base_store = pltpu.make_async_copy(base, base_o, store_sem.at[0])
    base_store.start()

    @on(0)
    def _():
        arrived(*sx2)
        arrived(zq)
        g_coup, r_coup, g_top = group_m[0], group_m[1], group_m[2]
        g_proj = zq_out[...] + zq_in[...]
        g_inv = spd_inverse(g_proj + g_coup)
        arrived(r1)
        block_rhs[...] = reduced[half] + r1_in[...]
        v_out[...] = dot(block_rhs[...], kept[1])
        begin(*r2)
        ft = dot(dot(g_inv, g_coup), g_top)
        ft_t = ft.T
        root_out[...] = r_coup + dot(ft_t, dot(g_proj, g_top))
        begin(*to_root)
        kept[3] = g_inv
        kept[4] = ft
        kept[5] = ft_t

    def again(c, carry):
        here = pl.ds(pl.multiple_of(c * HALF, HALF), HALF)
        resid[:, here] = resid[:, here] - stacked(pairs.at[0], sol[:, here])
        return carry

    lax.fori_loop(0, 2, again, 0)

    few_rows = pl.ds(pl.multiple_of(node * 32, 32), 32)
    r3 = [message(u_out, r3_in.at[d], ring[d], 0) for d in range(3)]
    r4 = [message(gout.at[few_rows], gout.at[few_rows], peers[d], 0) for d in range(7)]

    @on(0)
    def _():
        arrived(*r2)
        group_rhs = v_out[few_rows]
        for d in range(7):
            group_rhs = group_rhs + r2_in[d]
        u_out[...] = dot(group_rhs, kept[4])
        begin(*r3)
        part[...] = dot(group_rhs, kept[3])
        arrived(*to_root)
        r_inv = spd_inverse(root_out[...] + root_in[0] + root_in[1] + root_in[2])
        down = dot(r_inv, kept[5])
        arrived(*r3)
        root_rhs = u_out[...] + r3_in[0] + r3_in[1] + r3_in[2]
        gout[few_rows] = part[...] + dot(root_rhs, down)
        begin(*r4)

    def keep(ref, here, value):
        high, low = split(value)
        ref[0, :, here] = high
        ref[1, :, here] = low

    arrived(expand_in.high)

    @on(0)
    def _():
        arrived(expand_in.low)

    keep(out_o, pl.ds(0, RANK), expand[...])
    keep(cross_o, pl.ds(0, RANK), stacked(pairs.at[0], expand[...]))
    for k in range(2):
        keep(cross_o, pl.ds((k + 1) * RANK, RANK), stacked(pairs.at[k + 1], expand_halo[k]))

    def sides(c):
        here = cols(c)
        arrived(halo2_in[c].high)

        @on(0)
        def _():
            arrived(halo2_in[c].low)

        def side2(k, carry):
            resid[:, here] = resid[:, here] - stacked(pairs.at[k + 1], halo2[k, :, here])
            return carry

        lax.fori_loop(0, 2, side2, 0)

    r5 = message(block_own, block_out.at[half], mate_z, 0)
    r5_twin = message(block_own, block_out.at[half], twin, 0)
    r5_far = message(block_own, block_out.at[half], mate_z1, 0)
    k5 = counter[0]
    extra = [
        pltpu.make_async_remote_copy(
            src_ref=block_own,
            dst_ref=block_halo.at[half],
            send_sem=send_sem.at[k5 + way],
            recv_sem=recv_sem.at[k5 + zp],
            device_id=ahead[way],
            device_id_type=MESH,
        )
        for way in range(2)
    ]

    @on(0)
    def _():
        arrived(*r4)
        block_own[...] = dot(block_rhs[...], kept[0]) + dot(gout[...], kept[2])
        begin(r5, r5_far, r5_twin, *extra)
        block_out[half] = block_own[...]

    sides(0)
    sides(1)
    left_store = pltpu.make_async_copy(resid, left_o, store_sem.at[1])
    left_store.start()

    @on(0)
    def _():
        arrived(r5)

    @on(1)
    def _():
        arrived(r5_twin, r5_far)

    high, low = split(block_out[...].T)
    for k in range(3):
        node_o[0, pl.ds(k * RANK, RANK)] = high
        node_o[1, pl.ds(k * RANK, RANK)] = low

    def from_halo(k):
        for spot in range(2):
            pltpu.make_async_remote_copy(
                src_ref=block_own,
                dst_ref=block_halo.at[pl.ds(spot * 256, 256)],
                send_sem=send_sem.at[k5],
                recv_sem=recv_sem.at[k5 + spot],
                device_id=ahead[0],
                device_id_type=MESH,
            ).wait_recv()
        high, low = split(block_halo[...].T)
        node_o[0, pl.ds(k * RANK, RANK)] = high
        node_o[1, pl.ds(k * RANK, RANK)] = low

    @pl.when(j == 0)
    def _():
        from_halo(1)

    @pl.when(j == 3)
    def _():
        from_halo(2)

    for which in range(2):

        @on(which)
        def _():
            for copy in sent[which]:
                copy.wait_send()
            if which == 0:
                for copy in extra:
                    copy.wait_send()

    base_store.wait()
    left_store.wait()


def last_kernel(base_ref, left_ref, out_ref, cross_ref, node_ref, guess_ref, resid_ref):
    def three(left, count):
        return (
            plain(left[0], node_ref[0, :count])
            + plain(left[1], node_ref[0, :count])
            + plain(left[0], node_ref[1, :count])
        )

    guess_ref[...] = base_ref[...] - three(out_ref, RANK)
    resid_ref[...] = left_ref[...] + three(cross_ref, 3 * RANK)


def tree(*args):
    any_spec = pl.BlockSpec(memory_space=pl.ANY)
    vmem = pl.BlockSpec(memory_space=pltpu.VMEM)

    def buf(*shape, dtype=F32):
        return pltpu.VMEM(shape, dtype)

    scratch = [
        buf(4, LEAF, LEAF),
        buf(4, 2 * LEAF, LEAF, dtype=BF16),
        buf(LEAF, RHS),
        buf(LEAF, RHS),
        buf(LEAF, RHS),
        buf(LEAF, RHS),
        buf(LEAF, RHS),
        buf(2, LEAF, RHS),
        buf(2, LEAF, RHS),
        buf(LEAF, RANK),
        buf(RANK, RANK),
        buf(LEAF, RANK),
        buf(2, LEAF, RANK),
        buf(2 * RANK, LEAF, dtype=BF16),
        buf(5, RANK, RANK),
        buf(RANK, RANK),
        buf(RANK, RANK),
        buf(RANK, RANK),
        buf(5, RANK, RANK),
        buf(5, RANK, RANK),
        buf(2, RANK, RANK),
        buf(2, RANK, RANK),
        buf(3, 3, 32, RANK),
        buf(3, 32, RANK),
        buf(3, 3, 32, RANK),
        buf(3, RANK, RANK),
        buf(RANK, RANK),
        buf(3, RANK, RANK),
        buf(RANK, RANK),
        buf(RANK, RANK),
        buf(RANK, RANK),
        buf(3, RANK, RANK),
        buf(RHS, RANK),
        buf(RHS, RANK),
        buf(HALF, RANK),
        buf(6, RANK, RANK),
        buf(HALF, RANK),
        buf(HALF, RANK),
        buf(7, 32, RANK),
        buf(32, RANK),
        buf(3, 32, RANK),
        buf(32, RANK),
        buf(HALF, RANK),
        buf(HALF, RANK),
        buf(RHS, RANK),
        buf(RHS, RANK),
        pltpu.SemaphoreType.DMA((12,)),
        pltpu.SemaphoreType.DMA((2,)),
        pltpu.SemaphoreType.DMA((112,)),
        pltpu.SemaphoreType.DMA((112,)),
    ]
    base, left, out, cross, node = pl.pallas_call(
        tree_kernel,
        out_shape=[
            jax.ShapeDtypeStruct((LEAF, RHS), F32),
            jax.ShapeDtypeStruct((LEAF, RHS), F32),
            jax.ShapeDtypeStruct((2, LEAF, RANK), BF16),
            jax.ShapeDtypeStruct((2, LEAF, 3 * RANK), BF16),
            jax.ShapeDtypeStruct((2, 3 * RANK, RHS), BF16),
        ],
        in_specs=[any_spec] * 11,
        out_specs=[any_spec, any_spec, vmem, vmem, vmem],
        scratch_shapes=scratch,
        compiler_params=pltpu.CompilerParams(
            collective_id=0, has_side_effects=True, vmem_limit_bytes=56 * 2**20
        ),
    )(*args)
    block = 128
    return pl.pallas_call(
        last_kernel,
        grid=(LEAF // block,),
        in_specs=[
            pl.BlockSpec((block, RHS), lambda i: (i, 0)),
            pl.BlockSpec((block, RHS), lambda i: (i, 0)),
            pl.BlockSpec((2, block, RANK), lambda i: (0, i, 0)),
            pl.BlockSpec((2, block, 3 * RANK), lambda i: (0, i, 0)),
            pl.BlockSpec((2, 3 * RANK, RHS), lambda i: (0, 0, 0)),
        ],
        out_specs=[
            pl.BlockSpec((block, RHS), lambda i: (i, 0)),
            pl.BlockSpec((block, RHS), lambda i: (i, 0)),
        ],
        out_shape=[jax.ShapeDtypeStruct((LEAF, RHS), F32)] * 2,
    )(base, left, out, cross, node)


def body(
    right_side,
    guess,
    near_diag,
    near_lower,
    near_upper,
    leaf_inverse,
    leaf_basis,
    leaf_transfer,
    mid_share,
    top_share,
    coupling_share,
):
    new_guess, new_residual = tree(
        right_side,
        guess,
        near_diag[0],
        near_lower[0],
        near_upper[0],
        leaf_inverse[0],
        leaf_basis[0],
        leaf_transfer[0],
        mid_share[0],
        top_share[0],
        coupling_share[0],
    )
    return (new_guess, new_residual)


def solution(mesh):
    field = P(("grp", "leaf"), None)
    block = P(("grp", "leaf"), None, None)
    shares = P(("grp", "leaf"), None, None, None)
    in_specs = (field, field) + (block,) * 8 + (shares,)
    return jax.shard_map(
        body, mesh=mesh, in_specs=in_specs, out_specs=(field, field), check_vma=False
    )
```

```python
import jax
import jax.numpy as jnp
from jax import lax
from jax.experimental import pallas as pl
from jax.experimental.pallas import tpu as pltpu
from jax.sharding import PartitionSpec as P

MESH = pl.DeviceIdType.MESH
F32 = jnp.float32
BF16 = jnp.bfloat16
LEAF, RANK, RHS = 768, 128, 512
HALF = RHS // 2


def dot(left, right, over=(1, 0)):
    return lax.dot_general(
        left,
        right,
        (((over[0],), (over[1],)), ((), ())),
        precision=lax.Precision.HIGHEST,
        preferred_element_type=F32,
    )


def split(value):
    high = value.astype(BF16)
    return high, (value - high.astype(F32)).astype(BF16)


def plain(left, right, over=(1, 0)):
    return lax.dot_general(
        left, right, (((over[0],), (over[1],)), ((), ())), preferred_element_type=F32
    )


def stacked(pair_ref, value):
    count = pair_ref.shape[0] // 2
    high, low = split(value)
    both = plain(pair_ref[...], high)
    return both[:count] + both[count:] + plain(pair_ref[:count], low)


def spd_inverse(matrix):
    lane = lax.broadcasted_iota(jnp.int32, (8, 128), 1)
    sub = lax.broadcasted_iota(jnp.int32, (8, 128), 0)

    def total(t):
        return ((t[0] + t[1]) + (t[2] + t[3])) + ((t[4] + t[5]) + (t[6] + t[7]))

    def panel(rows, s):
        at = 8 * s
        head = (lane >= at) & (lane < at + 8)
        p = rows[s]
        sc = {}
        for k in range(8):
            col = jnp.broadcast_to(p[:, at + k : at + k + 1], (8, 128))
            for i in range(k + 1):
                sc[i, k] = jnp.broadcast_to(col[i : i + 1, :], (8, 128))

        def get(i, k):
            return sc[min(i, k), max(i, k)]

        for q in range(0, 8, 2):
            aa, bb, cc = sc[q, q], sc[q, q + 1], sc[q + 1, q + 1]
            det = aa * cc - bb * bb
            inv = pl.reciprocal(det, approx=True)
            inv = inv * (2.0 - det * inv)
            inv = inv * (2.0 - det * inv)
            ia, ib, ic = cc * inv, -bb * inv, aa * inv
            others = [i for i in range(8) if i not in (q, q + 1)]
            p0 = {i: get(i, q) for i in others}
            p1 = {i: get(i, q + 1) for i in others}
            q0 = {i: ia * p0[i] + ib * p1[i] for i in others}
            q1 = {i: ib * p0[i] + ic * p1[i] for i in others}
            for i in others:
                for k in others:
                    if i <= k:
                        sc[i, k] = sc[i, k] - (p0[i] * q0[k] + p1[i] * q1[k])
            for i in others:
                sc[min(i, q), max(i, q)] = q0[i]
                sc[min(i, q + 1), max(i, q + 1)] = q1[i]
            sc[q, q], sc[q, q + 1], sc[q + 1, q + 1] = -ia, -ib, -ic
        pm = jnp.where(head, jnp.where(lane == sub + at, -1.0, 0.0), p)
        pb = [jnp.broadcast_to(pm[m : m + 1, :], (8, 128)) for m in range(8)]
        nq = [total([get(k, m) * pb[m] for m in range(8)]) for k in range(8)]
        out = list(rows)
        for i in [(s + 1 + i) % 16 for i in range(15)]:
            r = rows[i]
            terms = [
                jnp.broadcast_to(r[:, at + k : at + k + 1], (8, 128)) * nq[k] for k in range(8)
            ]
            out[i] = jnp.where(head, 0.0, r) + total(terms)
        t = nq[7]
        for k in range(7):
            t = jnp.where(sub == k, nq[k], t)
        out[s] = -t
        return out

    def step(_, rows):
        rows = list(rows)
        for s in range(4):
            rows = panel(rows, s)
        rows = [pltpu.roll(r, 96, 1) for r in rows]
        return tuple(rows[4:] + rows[:4])

    rows = tuple(matrix[8 * i : 8 * i + 8, :] for i in range(16))
    rows = lax.fori_loop(0, 4, step, rows)
    return -jnp.concatenate(rows, 0)


def tree_kernel(
    right_h,
    guess_h,
    diag_h,
    lower_h,
    upper_h,
    inverse_h,
    basis_h,
    trans_h,
    mid_h,
    top_h,
    coup_h,
    base_o,
    left_o,
    out_o,
    cross_o,
    node_o,
    wide,
    pairs,
    right,
    guess,
    resid,
    sol,
    base,
    halo,
    halo2,
    basis,
    trans,
    expand,
    expand_halo,
    project,
    share,
    proj,
    proj_core,
    proj_z,
    chip,
    chip_in,
    pair_in,
    node_m,
    sx_in,
    sx_out,
    sz_in,
    group_m,
    q_out,
    xq_in,
    zq_out,
    zq_in,
    root_out,
    root_in,
    reduced,
    r1_in,
    v_out,
    r2_in,
    u_out,
    r3_in,
    gout,
    block_own,
    block_out,
    block_halo,
    load_sem,
    store_sem,
    send_sem,
    recv_sem,
):
    y = lax.axis_index("grp")
    l = lax.axis_index("leaf")
    core = l % 2
    j = l % 4
    z = (l // 2) % 4
    x = l // 8
    node = l // 4
    first = l - j
    index = y * 32 + l

    def at(place):
        place = place % 128
        return (place // 32, place % 32)

    nxt, prv = at(index + 1), at(index + 127)
    spots = [(j + d) % 4 for d in (1, 2, 3)]
    mates = [(y, first + spot) for spot in spots]
    twin = (y, l + 1 - 2 * core)
    mate_z = mates[1]
    x_spots = [(x + d) % 4 for d in (1, 2, 3)]
    cross = [(y, (l + 8 * d) % 32) for d in (1, 2, 3)]
    line = [(y, x * 8 + ((z + d) % 4) * 2 + core) for d in (1, 2, 3)]
    across_z = line[1]
    peers = [(y, (l + 4 * d) % 32) for d in range(1, 8)]
    peer_spots = [(node + d) % 8 for d in range(1, 8)]
    ring = [((y + d) % 4, l) for d in (1, 2, 3)]

    counter = [0]
    sent = []

    def remote(src, dst, device, start=True):
        k = counter[0]
        counter[0] += 1
        copy = pltpu.make_async_remote_copy(
            src_ref=src,
            dst_ref=dst,
            send_sem=send_sem.at[k],
            recv_sem=recv_sem.at[k],
            device_id=device,
            device_id_type=MESH,
        )
        if start:
            copy.start()
            sent.append(copy)
        return copy

    def arrived(*copies):
        for copy in copies:
            copy.wait_recv()

    local = []

    def load(src, dst):
        copy = pltpu.make_async_copy(src, dst, load_sem.at[len(local)])
        copy.start()
        local.append(copy)
        return copy

    load_share = [
        load(coup_h.at[0], share.at[0]),
        load(mid_h, share.at[1]),
        load(coup_h.at[pl.ds(1, 2)], share.at[pl.ds(2, 2)]),
        load(top_h, share.at[4]),
    ]
    load_inverse = load(inverse_h, wide.at[3])
    load_basis = load(basis_h, basis)
    load_trans = load(trans_h, trans)
    load_guess = load(guess_h, guess)
    load_diag = load(diag_h, wide.at[0])
    load_right = load(right_h, right)
    load_lower = load(lower_h, wide.at[1])
    load_upper = load(upper_h, wide.at[2])

    barrier = pltpu.get_barrier_semaphore()
    for device in [nxt, prv] + mates + peers + ring + line:
        pl.semaphore_signal(barrier, inc=1, device_id=device, device_id_type=MESH)

    @pl.when(j == 0)
    def _():
        for k in range(4):
            pl.semaphore_signal(
                barrier, inc=1, device_id=at(index + 124 + k), device_id_type=MESH
            )

    @pl.when(j == 3)
    def _():
        for k in range(4):
            pl.semaphore_signal(
                barrier, inc=1, device_id=at(index + 1 + k), device_id_type=MESH
            )

    pl.semaphore_wait(barrier, 20)

    def cols(c):
        return pl.ds(c * HALF, HALF)

    pieces = []

    def add_piece(src, dst, part):
        pieces.append(
            [
                remote(src.at[part], dst.at[(0,) + part], nxt, start=False),
                remote(src.at[part], dst.at[(1,) + part], prv, start=False),
            ]
        )
        return pieces[-1]

    def quarters(src, dst, c):
        return [add_piece(src, dst, (pl.ds(192 * q, 192), cols(c))) for q in range(4)]

    begun = [0]

    def pump(count):
        for _ in range(count):
            k = begun[0]
            if k >= 2:
                for copy in pieces[k - 2]:
                    copy.wait_send()
            for copy in pieces[k]:
                copy.start()
            begun[0] += 1

    halo_in = [quarters(guess_h, halo, c) for c in range(2)]
    expand_in = [
        add_piece(expand, expand_halo, (pl.ds(384 * q, 384), pl.ds(0, RANK))) for q in range(2)
    ]
    halo2_in = [quarters(sol, halo2, c) for c in range(2)]

    pump(2)

    for copy in load_share:
        copy.wait()
    half = pl.ds(pl.multiple_of(core * 64, 64), 64)
    other = pl.ds(pl.multiple_of(64 - core * 64, 64), 64)
    e1 = remote(share.at[:, other], chip_in, twin)

    def divide(m, scale=None):
        value = wide[m]
        if scale is not None:
            value = value * scale
        high, low = split(value)
        pairs[m, pl.ds(0, LEAF)] = high
        pairs[m, pl.ds(LEAF, LEAF)] = low

    load_inverse.wait()
    load_basis.wait()
    load_trans.wait()
    basis_t = basis[...].T
    trans_t = trans[...].T
    weighted = dot(wide[3], basis[...])
    proj[...] = dot(trans_t, dot(dot(basis_t, weighted), trans[...]))
    e_core = remote(proj, proj_core, twin)

    arrived(e1)
    chip[...] = share[:, half] + chip_in[...]
    e_pair = remote(chip.at[pl.ds(0, 2)], pair_in, mate_z)
    sx = [
        remote(chip.at[pl.ds(2, 3), pl.ds(x_spots[d] * 16, 16)], sx_in.at[d], cross[d])
        for d in range(3)
    ]
    arrived(e_core)
    proj_core[...] = proj[...] + proj_core[...]
    e_z = remote(proj_core, proj_z, mate_z)
    pump(2)

    expand[...] = dot(weighted, trans[...])
    high, low = split(dot(trans_t, basis_t))
    project[pl.ds(0, RANK)] = high
    project[pl.ds(RANK, RANK)] = low

    load_guess.wait()
    load_diag.wait()
    load_right.wait()
    divide(0)

    def own(c, carry):
        here = pl.ds(pl.multiple_of(c * HALF, HALF), HALF)
        resid[:, here] = right[:, here] - stacked(pairs.at[0], guess[:, here])
        return carry

    lax.fori_loop(0, 2, own, 0)

    arrived(e_pair)
    node_m[:, half] = chip[0:2] + pair_in[...]
    e_half = remote(node_m.at[:, half], node_m.at[:, half], twin)
    arrived(*sx)
    sx_own = pl.ds(pl.multiple_of(x * 16, 16), 16)
    sx_out[...] = chip[2:5, sx_own] + sx_in[0] + sx_in[1] + sx_in[2]
    sz = [remote(sx_out, sz_in.at[d], line[d]) for d in range(3)]
    arrived(e_z)
    arrived(e_half)
    p_proj, p_coup, p_mid = proj_core[...] + proj_z[...], node_m[0], node_m[1]
    pump(2)
    p_inv = spd_inverse(p_proj + p_coup)
    fm = dot(dot(p_inv, p_coup), p_mid)
    mf = fm.T
    q_out[...] = dot(mf, dot(p_proj, p_mid))
    xq = [remote(q_out.at[half], xq_in.at[d], cross[d]) for d in range(3)]

    arrived(*sz)
    group_rows = pl.ds(pl.multiple_of(core * 64 + x * 16, 16), 16)
    group_m[pl.ds(0, 3), group_rows] = sx_out[...] + sz_in[0] + sz_in[1] + sz_in[2]
    sx2 = [
        remote(group_m.at[pl.ds(0, 3), group_rows], group_m.at[pl.ds(0, 3), group_rows], cross[d])
        for d in range(3)
    ]
    pump(2)

    load_lower.wait()
    load_upper.wait()
    divide(1, jnp.where(index == 0, 0.0, 1.0))
    divide(2, jnp.where(index == 127, 0.0, 1.0))
    divide(3)

    def leaf_chunk(c):
        here = cols(c)
        for pair in halo_in[c]:
            arrived(*pair)

        def side(k, carry):
            resid[:, here] = resid[:, here] - stacked(pairs.at[k + 1], halo[k, :, here])
            return carry

        lax.fori_loop(0, 2, side, 0)
        sol[:, here] = stacked(pairs.at[3], resid[:, here])

    def reduce_chunk(c):
        here = cols(c)
        reduced[here, :] = stacked(project, sol[:, here]).T

    leaf_chunk(0)

    arrived(*xq)
    zq_out[...] = q_out[half] + xq_in[0] + xq_in[1] + xq_in[2]
    zq = remote(zq_out, zq_in, across_z)
    arrived(*sx2)
    s_half = remote(group_m.at[pl.ds(0, 3), half], group_m.at[pl.ds(0, 3), half], twin)
    pump(2)
    reduce_chunk(0)
    base[:, cols(0)] = guess[:, cols(0)] + sol[:, cols(0)]

    pump(1)
    leaf_chunk(1)
    reduce_chunk(1)
    r1 = [remote(reduced.at[pl.ds(spots[d] * 128, 128)], r1_in.at[d], mates[d]) for d in range(3)]
    pump(2)
    arrived(zq)
    group_m[3, half] = zq_out[...] + zq_in[...]
    g_half = remote(group_m.at[3, half], group_m.at[3, half], twin)
    base[:, cols(1)] = guess[:, cols(1)] + sol[:, cols(1)]
    base_store = pltpu.make_async_copy(base, base_o, store_sem.at[0])
    base_store.start()

    arrived(s_half, g_half)
    g_coup, r_coup, g_top, g_proj = group_m[0], group_m[1], group_m[2], group_m[3]
    g_inv = spd_inverse(g_proj + g_coup)

    arrived(*r1)
    wide_rows = pl.ds(pl.multiple_of(j * 128, 128), 128)
    block_rhs = reduced[wide_rows] + r1_in[0] + r1_in[1] + r1_in[2]
    v_out[...] = dot(block_rhs, fm)
    r2 = [
        remote(v_out.at[pl.ds(peer_spots[d] * 16, 16)], r2_in.at[d], peers[d]) for d in range(7)
    ]
    ft = dot(dot(g_inv, g_coup), g_top)
    ft_t = ft.T
    root_out[...] = r_coup + dot(ft_t, dot(g_proj, g_top))
    to_root = [remote(root_out, root_in.at[d], ring[d]) for d in range(3)]
    pump(2)
    block_part = dot(block_rhs, p_inv)

    def again(c, carry):
        here = pl.ds(pl.multiple_of(c * HALF, HALF), HALF)
        resid[:, here] = resid[:, here] - stacked(pairs.at[0], sol[:, here])
        return carry

    lax.fori_loop(0, 2, again, 0)

    arrived(*r2)
    few_rows = pl.ds(pl.multiple_of(node * 16, 16), 16)
    group_rhs = v_out[few_rows]
    for d in range(7):
        group_rhs = group_rhs + r2_in[d]
    u_out[...] = dot(group_rhs, ft)
    r3 = [remote(u_out, r3_in.at[d], ring[d]) for d in range(3)]
    pump(2)
    group_part = dot(group_rhs, g_inv)

    arrived(*to_root)
    r_inv = spd_inverse(root_out[...] + root_in[0] + root_in[1] + root_in[2])
    down = dot(r_inv, ft_t)

    arrived(*r3)
    root_rhs = u_out[...] + r3_in[0] + r3_in[1] + r3_in[2]
    gout[few_rows] = group_part + dot(root_rhs, down)
    r4 = [remote(gout.at[few_rows], gout.at[few_rows], peers[d]) for d in range(7)]
    pump(1)

    def keep(ref, here, value):
        high, low = split(value)
        ref[0, :, here] = high
        ref[1, :, here] = low

    for pair in expand_in:
        arrived(*pair)
    every = pl.ds(0, RANK)
    keep(out_o, every, expand[...])
    keep(cross_o, every, stacked(pairs.at[0], expand[...]))
    for k in range(2):
        keep(cross_o, pl.ds((k + 1) * RANK, RANK), stacked(pairs.at[k + 1], expand_halo[k]))

    def sides(c):
        here = cols(c)
        for pair in halo2_in[c]:
            arrived(*pair)

        def side2(k, carry):
            resid[:, here] = resid[:, here] - stacked(pairs.at[k + 1], halo2[k, :, here])
            return carry

        lax.fori_loop(0, 2, side2, 0)

    sides(0)

    arrived(*r4)
    block_own[...] = block_part + dot(gout[...], mf)
    block_out[wide_rows] = block_own[...]
    r5 = [remote(block_own, block_out.at[wide_rows], mates[d]) for d in range(3)]
    k5 = counter[0]
    ahead = [at(index - j + 4), at(index - j + 127)]
    extra = [
        pltpu.make_async_remote_copy(
            src_ref=block_own,
            dst_ref=block_halo.at[wide_rows],
            send_sem=send_sem.at[k5 + way],
            recv_sem=recv_sem.at[k5 + 2 + j],
            device_id=ahead[way],
            device_id_type=MESH,
        )
        for way in range(2)
    ]
    for copy in extra:
        copy.start()

    sides(1)
    left_store = pltpu.make_async_copy(resid, left_o, store_sem.at[1])
    left_store.start()

    arrived(*r5)
    high, low = split(block_out[...].T)
    for k in range(3):
        node_o[0, pl.ds(k * RANK, RANK)] = high
        node_o[1, pl.ds(k * RANK, RANK)] = low

    def from_halo(k):
        for spot in range(4):
            pltpu.make_async_remote_copy(
                src_ref=block_own,
                dst_ref=block_halo.at[pl.ds(spot * 128, 128)],
                send_sem=send_sem.at[k5],
                recv_sem=recv_sem.at[k5 + 2 + spot],
                device_id=ahead[0],
                device_id_type=MESH,
            ).wait_recv()
        high, low = split(block_halo[...].T)
        node_o[0, pl.ds(k * RANK, RANK)] = high
        node_o[1, pl.ds(k * RANK, RANK)] = low

    @pl.when(j == 0)
    def _():
        from_halo(1)

    @pl.when(j == 3)
    def _():
        from_halo(2)

    for pair in pieces[-2:]:
        for copy in pair:
            copy.wait_send()
    for copy in sent + extra:
        copy.wait_send()
    base_store.wait()
    left_store.wait()


def last_kernel(base_ref, left_ref, out_ref, cross_ref, node_ref, guess_ref, resid_ref):
    def three(left, count):
        return (
            plain(left[0], node_ref[0, :count])
            + plain(left[1], node_ref[0, :count])
            + plain(left[0], node_ref[1, :count])
        )

    guess_ref[...] = base_ref[...] - three(out_ref, RANK)
    resid_ref[...] = left_ref[...] + three(cross_ref, 3 * RANK)


def tree(*args):
    any_spec = pl.BlockSpec(memory_space=pl.ANY)
    vmem = pl.BlockSpec(memory_space=pltpu.VMEM)

    def buf(*shape, dtype=F32):
        return pltpu.VMEM(shape, dtype)

    scratch = [
        buf(4, LEAF, LEAF),
        buf(4, 2 * LEAF, LEAF, dtype=BF16),
        buf(LEAF, RHS),
        buf(LEAF, RHS),
        buf(LEAF, RHS),
        buf(LEAF, RHS),
        buf(LEAF, RHS),
        buf(2, LEAF, RHS),
        buf(2, LEAF, RHS),
        buf(LEAF, RANK),
        buf(RANK, RANK),
        buf(LEAF, RANK),
        buf(2, LEAF, RANK),
        buf(2 * RANK, LEAF, dtype=BF16),
        buf(5, RANK, RANK),
        buf(RANK, RANK),
        buf(RANK, RANK),
        buf(RANK, RANK),
        buf(5, 64, RANK),
        buf(5, 64, RANK),
        buf(2, 64, RANK),
        buf(2, RANK, RANK),
        buf(3, 3, 16, RANK),
        buf(3, 16, RANK),
        buf(3, 3, 16, RANK),
        buf(4, RANK, RANK),
        buf(RANK, RANK),
        buf(3, 64, RANK),
        buf(64, RANK),
        buf(64, RANK),
        buf(RANK, RANK),
        buf(3, RANK, RANK),
        buf(RHS, RANK),
        buf(3, RANK, RANK),
        buf(RANK, RANK),
        buf(7, 16, RANK),
        buf(16, RANK),
        buf(3, 16, RANK),
        buf(RANK, RANK),
        buf(RANK, RANK),
        buf(RHS, RANK),
        buf(RHS, RANK),
        pltpu.SemaphoreType.DMA((12,)),
        pltpu.SemaphoreType.DMA((2,)),
        pltpu.SemaphoreType.DMA((96,)),
        pltpu.SemaphoreType.DMA((96,)),
    ]
    base, left, out, cross, node = pl.pallas_call(
        tree_kernel,
        out_shape=[
            jax.ShapeDtypeStruct((LEAF, RHS), F32),
            jax.ShapeDtypeStruct((LEAF, RHS), F32),
            jax.ShapeDtypeStruct((2, LEAF, RANK), BF16),
            jax.ShapeDtypeStruct((2, LEAF, 3 * RANK), BF16),
            jax.ShapeDtypeStruct((2, 3 * RANK, RHS), BF16),
        ],
        in_specs=[any_spec] * 11,
        out_specs=[any_spec, any_spec, vmem, vmem, vmem],
        scratch_shapes=scratch,
        compiler_params=pltpu.CompilerParams(
            collective_id=0, has_side_effects=True, vmem_limit_bytes=56 * 2**20
        ),
    )(*args)
    block = 256
    return pl.pallas_call(
        last_kernel,
        grid=(LEAF // block,),
        in_specs=[
            pl.BlockSpec((block, RHS), lambda i: (i, 0)),
            pl.BlockSpec((block, RHS), lambda i: (i, 0)),
            pl.BlockSpec((2, block, RANK), lambda i: (0, i, 0)),
            pl.BlockSpec((2, block, 3 * RANK), lambda i: (0, i, 0)),
            pl.BlockSpec((2, 3 * RANK, RHS), lambda i: (0, 0, 0)),
        ],
        out_specs=[
            pl.BlockSpec((block, RHS), lambda i: (i, 0)),
            pl.BlockSpec((block, RHS), lambda i: (i, 0)),
        ],
        out_shape=[jax.ShapeDtypeStruct((LEAF, RHS), F32)] * 2,
    )(base, left, out, cross, node)


def body(
    right_side,
    guess,
    near_diag,
    near_lower,
    near_upper,
    leaf_inverse,
    leaf_basis,
    leaf_transfer,
    mid_share,
    top_share,
    coupling_share,
):
    new_guess, new_residual = tree(
        right_side,
        guess,
        near_diag[0],
        near_lower[0],
        near_upper[0],
        leaf_inverse[0],
        leaf_basis[0],
        leaf_transfer[0],
        mid_share[0],
        top_share[0],
        coupling_share[0],
    )
    return (new_guess, new_residual)


def solution(mesh):
    field = P(("grp", "leaf"), None)
    block = P(("grp", "leaf"), None, None)
    shares = P(("grp", "leaf"), None, None, None)
    in_specs = (field, field) + (block,) * 8 + (shares,)
    return jax.shard_map(
        body, mesh=mesh, in_specs=in_specs, out_specs=(field, field), check_vma=False
    )
```
